32 devices in a mesh: grp: 4 (over y, x), col: 8 (over z, core).
Axes of the slice: x: 2, y: 2, z: 4, core: 2. Of those that a mesh axis runs over, the one named last changes fastest.
Arguments:
- orbitals: bfloat16 [2, 6656, 4096], P(None, 'col', 'grp'), may hold values from -6 to 6
- cosine_tiles: bfloat16 [32, 256, 256], P(('grp', 'col')), may hold values from -0.125 to 0.125
- sine_tiles: bfloat16 [32, 256, 256], P(('grp', 'col')), may hold values from -0.125 to 0.125
- tile_row: int32 [32], P('grp'), may hold values from -1 to 3, as said below
- tile_col: int32 [32], P('grp'), may hold values from -1 to 15, as said below
- row_place: int32 [16], replicated, may hold values from 0 to 15, each once
Outputs:
- propagated: bfloat16 [2, 6656, 4096], P(None, 'col', 'grp')
The draws below stay inside these ranges and needn't reach their ends.
Inputs may be any that keep to these rules, and one draw needn't show every extreme that they name: `tile_row`: slot t belongs to group t // 8; a used slot names one of the group's 4 block rows; empty slots are -1 here and in tile_col at the same places; every group uses two fifths of its 8 slots or more, some group all of them, and a group's used slots lie anywhere among its slots. Two slots may name the same tile position, and their tiles then add. `tile_col`: A used slot names any initial block column of the slab. Initial block row p is stored as storage block row_place[p], in group row_place[p] // 4.
All inputs are finite; a program needn't handle non-finite values.
Results may differ from the reference program's by a relative error of at most 0.005.
Values may be sent and summed in bfloat16 or wider, within the bound.
A program may use at most 128 MiB of HBM per device.

```python
import jax
import jax.numpy as jnp
from jax import lax

TILE = 256
ORB = 6656
RPG = 4
STEPS = 2
GCAP = 8
NB = 16
NROWS = 4096
N_GRP = 4


def group_ranking(subkey):
    return jax.random.permutation(subkey, GCAP)


def tile_lists(key):
    folded = jax.random.fold_in(key, 31)
    count_key, full_key, rank_key, row_key, col_key = jax.random.split(folded, 5)
    counts = jax.random.randint(count_key, (N_GRP,), (2 * GCAP + 4) // 5, GCAP + 1)
    full_group = jax.random.randint(full_key, (), 0, N_GRP)
    counts = jnp.where(jnp.arange(N_GRP) == full_group, GCAP, counts)
    ranking = jax.vmap(group_ranking)(jax.random.split(rank_key, N_GRP))
    occupied = ranking < counts[:, None]
    row_draw = jax.random.randint(row_key, (N_GRP, GCAP), 0, RPG)
    col_draw = jax.random.randint(col_key, (N_GRP, GCAP), 0, NB)
    rows_out = jnp.where(occupied, row_draw, -1).reshape(N_GRP * GCAP).astype(jnp.int32)
    cols_out = jnp.where(occupied, col_draw, -1).reshape(N_GRP * GCAP).astype(jnp.int32)
    return (rows_out, cols_out)


def draw_tile_row(key, part):
    return tile_lists(key)[0]


def draw_tile_col(key, part):
    return tile_lists(key)[1]


def shard_levels(stream_key, extent, shards, least, high):
    loudness, own = 1.0, jax.random.fold_in(stream_key, 6)
    for dim, parts in shards:
        draws = jnp.exp(jax.random.uniform(jax.random.fold_in(own, dim), (parts,), jnp.float32, least / len(shards), high / len(shards)))
        loudness = loudness * jnp.repeat(draws, extent[dim] // parts).reshape([-1 if axis == dim else 1 for axis in range(len(extent))])
    return loudness


def centred(key, dims, scale, most, shards=(), held_as=jnp.bfloat16):
    factor_of = shard_levels(key, dims, shards, -0.22, 0.18) if shards else 1.0
    array = jax.random.normal(key, dims, jnp.float32) * scale * factor_of
    return jnp.minimum(jnp.maximum(array, -most), most).astype(held_as)


def setup_inputs(seed: int = 0) -> dict:
    keys = jax.random.split(jax.random.key(seed), 7)
    return {
        "orbitals": centred(keys[0], (2, ORB, NROWS), 1.0, 6.0, ((1, 8), (2, 4))),
        "cosine_tiles": centred(keys[1], (N_GRP * GCAP, TILE, TILE), (4 * GCAP * TILE // RPG) ** -0.5, 0.125, ((0, 32),)),
        "sine_tiles": centred(keys[2], (N_GRP * GCAP, TILE, TILE), (4 * GCAP * TILE // RPG) ** -0.5, 0.125, ((0, 32),)),
        "tile_row": draw_tile_row(jax.random.fold_in(keys[6], 71), 0),
        "tile_col": draw_tile_col(jax.random.fold_in(keys[6], 71), 0),
        "row_place": jax.random.permutation(keys[5], NB).astype(jnp.int32),
    }


def apply_tiles(panels, tiles, tile_row, source_block):
    def one_group(group_data):
        group_tiles, group_rows, group_source = group_data
        chosen = jnp.take(panels, group_source, axis=1).astype(jnp.float32)
        product = jnp.einsum("osj,sij->osi", chosen, group_tiles.astype(jnp.float32), precision=lax.Precision.HIGHEST)
        onehot = (group_rows[:, None] == jnp.arange(RPG, dtype=jnp.int32)[None, :]).astype(jnp.float32)
        return jnp.einsum("osi,sr->ori", product, onehot, precision=lax.Precision.HIGHEST)

    stacked = lax.map(one_group, (tiles.reshape(N_GRP, GCAP, TILE, TILE), tile_row.reshape(N_GRP, GCAP), source_block.reshape(N_GRP, GCAP)))
    return jnp.transpose(stacked, (1, 0, 2, 3)).reshape(stacked.shape[1], NB, TILE)


def reference(orbitals, cosine_tiles, sine_tiles, tile_row, tile_col, row_place):
    source_block = jnp.where(tile_col >= 0, jnp.take(row_place, jnp.clip(tile_col, 0, NB - 1)), 0).astype(jnp.int32)
    current = orbitals.reshape(2 * ORB, NB, TILE)
    for update in range(STEPS):
        spread = apply_tiles(current, cosine_tiles, tile_row, source_block).astype(jnp.bfloat16)
        cosine_part = apply_tiles(spread, cosine_tiles, tile_row, source_block)
        sine_part = apply_tiles(spread, sine_tiles, tile_row, source_block)
        previous = current.astype(jnp.float32)
        real_new = 2.0 * (cosine_part[:ORB] + sine_part[ORB:]) - previous[:ORB]
        imag_new = 2.0 * (cosine_part[ORB:] - sine_part[:ORB]) - previous[ORB:]
        current = jnp.concatenate([real_new, imag_new], axis=0).astype(jnp.bfloat16)
    return current.reshape(2, ORB, NROWS)
```

```python
import functools

import jax
import jax.numpy as jnp
from jax import lax
from jax.experimental import pallas as pl
from jax.experimental.pallas import tpu as pltpu
from jax.sharding import PartitionSpec as P

STEPS = 2
ROW_TILE = 16
CHUNKS = 2
MESH = pl.DeviceIdType.MESH
VMEM_LIMIT = 48 * 2**20


def row_sums(product, rows_onehot):
    group_rows = rows_onehot.shape[1]
    totals = [
        jnp.sum(product * rows_onehot[:, row_number][None, :, None], axis=1)
        for row_number in range(group_rows)
    ]
    return jnp.stack(totals, axis=1)


def tile_product(panels, tiles, rows_onehot, source):
    chosen = jnp.take(panels, source, axis=1)
    product = jnp.einsum("osj,sij->osi", chosen, tiles, preferred_element_type=jnp.float32)
    return row_sums(product, rows_onehot)


def find_source(tile_col, row_place):
    blocks = jnp.arange(row_place.shape[0], dtype=jnp.int32)
    return jnp.sum(jnp.where(tile_col[:, None] == blocks[None, :], row_place[None, :], 0), axis=1)


def gather_plan(orbitals, cosine_tiles, sine_tiles, tile_row, tile_col, row_place):
    halves, orbital_count, rows_dev = orbitals.shape
    tile_size = cosine_tiles.shape[-1]
    group_rows = rows_dev // tile_size
    slab_blocks = row_place.shape[0]
    columns = halves * orbital_count
    source = find_source(tile_col, row_place)
    rows_onehot = (tile_row[:, None] == jnp.arange(group_rows, dtype=jnp.int32)[None, :]).astype(
        jnp.float32
    )
    current = orbitals
    cosine_all = lax.all_gather(cosine_tiles, "col", axis=0, tiled=True)
    sine_all = lax.all_gather(sine_tiles, "col", axis=0, tiled=True)
    for _ in range(STEPS):
        panels = lax.all_gather(current, "grp", axis=2, tiled=True).reshape(
            columns, slab_blocks, tile_size
        )
        direct = tile_product(panels, cosine_all, rows_onehot, source)
        spread = direct.astype(jnp.bfloat16).reshape(halves, orbital_count, rows_dev)
        spread_all = lax.all_gather(spread, "grp", axis=2, tiled=True).reshape(
            columns, slab_blocks, tile_size
        )
        cosine_part = tile_product(spread_all, cosine_all, rows_onehot, source)
        sine_part = tile_product(spread_all, sine_all, rows_onehot, source)
        previous = current.astype(jnp.float32).reshape(columns, group_rows, tile_size)
        real_new = (
            2.0 * (cosine_part[:orbital_count] + sine_part[orbital_count:])
            - previous[:orbital_count]
        )
        imag_new = (
            2.0 * (cosine_part[orbital_count:] - sine_part[:orbital_count])
            - previous[orbital_count:]
        )
        current = (
            jnp.concatenate([real_new, imag_new], axis=0)
            .astype(jnp.bfloat16)
            .reshape(halves, orbital_count, rows_dev)
        )
    return current


def slot_lists(tile_row, tile_col, row_place, group_rows):
    slots = tile_row.shape[0]
    number = jnp.arange(slots, dtype=jnp.int32)
    row = jnp.where(tile_row < 0, group_rows, tile_row)
    key = row * slots + number
    rank = jnp.sum((key[None, :] < key[:, None]).astype(jnp.int32), axis=1)
    place = (rank[None, :] == number[:, None]).astype(jnp.int32)
    source = find_source(tile_col, row_place)
    order = jnp.sum(place * number[None, :], axis=1)
    sorted_source = jnp.sum(place * source[None, :], axis=1)
    sorted_row = jnp.sum(place * row[None, :], axis=1)
    before = jnp.concatenate([jnp.full((1,), -1, jnp.int32), sorted_row[:-1]])
    keep = (sorted_row == before).astype(jnp.int32)
    rows = jnp.arange(group_rows, dtype=jnp.int32)
    last = jnp.maximum(jnp.sum((row[None, :] <= rows[:, None]).astype(jnp.int32), axis=1) - 1, 0)
    used = jnp.max((row[None, :] == rows[:, None]).astype(jnp.int32), axis=1)
    table = [order, sorted_source, keep, last, used]
    table = [jnp.pad(line, (0, 128 - line.shape[0])) for line in table]
    return jnp.pad(jnp.stack(table), ((0, 8 - len(table)), (0, 0)))


def dot_t(panel, tile):
    return lax.dot_general(
        panel, tile, (((1,), (1,)), ((), ())), preferred_element_type=jnp.float32
    )


def propagate(current, spread, sums, cosine, sine, table, n_grp, group_rows, slots):
    halves, length, tile_size = current.shape[1:]
    height = halves * length

    def slot_values(g, k):
        return table[g, 0, k], table[g, 1, k], table[g, 2, k].astype(jnp.float32)

    def spread_group(g, carry):
        total = None
        for k in range(slots):
            slot, source, keep = slot_values(g, k)
            panel = current[source].reshape(height, tile_size)
            product = dot_t(panel, cosine[g, slot])
            total = product if k == 0 else product + total * keep
            sums[k, :height] = total
        for r in range(group_rows):
            used = table[g, 4, r].astype(jnp.float32)
            spread[g * group_rows + r, :height] = (sums[table[g, 3, r], :height] * used).astype(
                spread.dtype
            )
        return carry

    def double_group(g, carry):
        total = None
        for k in range(slots):
            slot, source, keep = slot_values(g, k)
            panel = spread[source, :height]
            by_cosine = dot_t(panel, cosine[g, slot])
            by_sine = dot_t(panel, sine[g, slot])
            product = jnp.concatenate(
                [by_cosine[:length] + by_sine[length:], by_cosine[length:] - by_sine[:length]],
                axis=0,
            )
            total = product if k == 0 else product + total * keep
            sums[k, :height] = total
        for r in range(group_rows):
            used = table[g, 4, r].astype(jnp.float32)
            block = g * group_rows + r
            previous = current[block].reshape(height, tile_size).astype(jnp.float32)
            new = 2.0 * (sums[table[g, 3, r], :height] * used) - previous
            current[block] = new.astype(current.dtype).reshape(halves, length, tile_size)
        return carry

    def step(_, carry):
        lax.fori_loop(0, n_grp, spread_group, 0)
        lax.fori_loop(0, n_grp, double_group, 0)
        return carry

    lax.fori_loop(0, STEPS, step, 0)


def kernel(n_grp, n_z, cuts, group_rows, orb, cos_in, sin_in, lists, out, *scratch):
    currents = scratch[: len(cuts)]
    (
        spread,
        sums,
        cosine,
        sine,
        table_v,
        table,
        list_send,
        list_recv,
        table_sem,
        lane_send,
        lane_recv,
        pair_send,
        pair_recv,
        own_sem,
        in_send,
        in_recv,
        in_local,
        out_send,
        out_recv,
        out_local,
    ) = scratch[len(cuts) :]
    tile_size = cosine.shape[-1]
    slots = cosine.shape[1]
    share = orb.shape[1] // n_grp
    grp, col = lax.axis_index("grp"), lax.axis_index("col")
    z, core = col // 2, col % 2
    tiles = (cosine, sine)
    own = (cos_in.at[0], sin_in.at[0])

    def grp_at(shift):
        return lax.rem(grp + shift + n_grp, n_grp)

    def z_at(shift):
        return lax.rem(z + shift + n_z, n_z)

    def device(dg, dz):
        return (grp_at(dg), z_at(dz) * 2 + core)

    pair = (grp, z * 2 + 1 - core)
    sent = []

    def remote(src, dst, send_sem, recv_sem, to):
        return pltpu.make_async_remote_copy(
            src_ref=src,
            dst_ref=dst,
            send_sem=send_sem,
            recv_sem=recv_sem,
            device_id=to,
            device_id_type=MESH,
        )

    def start(copy):
        copy.start()
        sent.append(copy)

    barrier = pltpu.get_barrier_semaphore()
    partners = [device(s, 0) for s in range(1, n_grp)]
    partners += [device(0, s) for s in range(1, n_z)] + [pair]
    for partner in partners:
        pl.semaphore_signal(barrier, inc=1, device_id=partner, device_id_type=MESH)
    pl.semaphore_wait(barrier, len(partners))

    def tile_ref(k, tg, tz, lane):
        return tiles[k].at[grp_at(-tg), z_at(-tz) * 2 + lane]

    def lane_copy(k, tg, tz, dg, dz):
        dst = tile_ref(k, tg, tz, core)
        src = own[k] if (tg, tz) == (0, 0) else dst
        at = (k, tg + dg, tz + dz)
        start(remote(src, dst, lane_send.at[at], lane_recv.at[at], device(dg, dz)))

    def lane_wait(k, sg, sz):
        ref = tile_ref(k, sg, sz, core)
        at = (k, sg, sz)
        remote(ref, ref, lane_send.at[at], lane_recv.at[at], pair).wait_recv()

    def pair_copy(k, sg, sz):
        dst = tile_ref(k, sg, sz, core)
        src = own[k] if (sg, sz) == (0, 0) else dst
        at = (k, sg, sz)
        start(remote(src, dst, pair_send.at[at], pair_recv.at[at], pair))

    def pair_wait(k, sg, sz):
        ref = tile_ref(k, sg, sz, 1 - core)
        at = (k, sg, sz)
        remote(ref, ref, pair_send.at[at], pair_recv.at[at], pair).wait_recv()

    for s in range(1, n_grp):
        start(remote(lists, table_v.at[grp], list_send.at[s], list_recv.at[s], device(s, 0)))
    for s in range(1, n_z):
        lane_copy(0, 0, 0, 0, s)
    for s in range(1, n_grp):
        lane_copy(1, 0, 0, s, 0)
    local = [pltpu.make_async_copy(lists, table_v.at[grp], own_sem.at[2])]
    for k in range(2):
        local.append(pltpu.make_async_copy(own[k], tile_ref(k, 0, 0, core), own_sem.at[k]))
    for copy in local:
        copy.start()
    for k in range(2):
        pair_copy(k, 0, 0)
    for s in range(1, n_grp):
        lane_copy(0, 0, 0, s, 0)
    for s in range(1, n_z):
        lane_copy(1, 0, 0, 0, s)

    def in_piece(c, s, r):
        begin, length = cuts[c]
        rows = pl.ds(pl.multiple_of(grp_at(s) * share + begin, ROW_TILE), length)
        src = orb.at[:, rows, pl.ds(r * tile_size, tile_size)]
        return src, currents[c].at[grp * group_rows + r]

    for c in range(len(cuts)):
        for r in range(group_rows):
            src, dst = in_piece(c, 0, r)
            pltpu.make_async_copy(src, dst, in_local.at[c, r]).start()
            for s in range(1, n_grp):
                src, dst = in_piece(c, s, r)
                at = (c, s, r)
                start(remote(src, dst, in_send.at[at], in_recv.at[at], device(s, 0)))

    for s in range(1, max(n_grp, n_z)):
        if s < n_z:
            lane_wait(0, 0, s)
            for d in range(1, n_grp):
                lane_copy(0, 0, s, d, 0)
            pair_copy(0, 0, s)
        if s < n_grp:
            lane_wait(1, s, 0)
            for d in range(1, n_z):
                lane_copy(1, s, 0, 0, d)
            pair_copy(1, s, 0)
    for sz in range(n_z):
        for sg in range(1, n_grp):
            lane_wait(0, sg, sz)
            pair_copy(0, sg, sz)
    for sg in range(n_grp):
        for sz in range(1, n_z):
            lane_wait(1, sg, sz) if sg or sz else None
            pair_copy(1, sg, sz)
    for copy in local:
        copy.wait()
    for s in range(1, n_grp):
        ref = table_v.at[grp_at(-s)]
        remote(ref, ref, list_send.at[s], list_recv.at[s], pair).wait_recv()
    to_scalar = pltpu.make_async_copy(table_v, table, table_sem.at[0])
    to_scalar.start()
    to_scalar.wait()
    for k in range(2):
        for sg in range(n_grp):
            for sz in range(n_z):
                pair_wait(k, sg, sz)

    def out_piece(c, s, r):
        begin, length = cuts[c]
        rows = pl.ds(pl.multiple_of(grp * share + begin, ROW_TILE), length)
        dst = out.at[:, rows, pl.ds(r * tile_size, tile_size)]
        return currents[c].at[grp_at(s) * group_rows + r], dst

    def landing(c, s, r):
        begin, length = cuts[c]
        rows = pl.ds(pl.multiple_of(grp_at(-s) * share + begin, ROW_TILE), length)
        return out.at[:, rows, pl.ds(r * tile_size, tile_size)]

    for c in range(len(cuts)):
        for r in range(group_rows):
            src, dst = in_piece(c, 0, r)
            pltpu.make_async_copy(src, dst, in_local.at[c, r]).wait()
            for s in range(1, n_grp):
                ref = currents[c].at[grp_at(-s) * group_rows + r]
                at = (c, s, r)
                remote(ref, ref, in_send.at[at], in_recv.at[at], pair).wait_recv()
        propagate(
            currents[c], spread, sums, cosine, sine, table, n_grp, group_rows, slots
        )
        for r in range(group_rows):
            for s in range(1, n_grp):
                src, dst = out_piece(c, s, r)
                at = (c, s, r)
                start(remote(src, dst, out_send.at[at], out_recv.at[at], device(s, 0)))
            src, dst = out_piece(c, 0, r)
            pltpu.make_async_copy(src, dst, out_local.at[c, r]).start()
    for c in range(len(cuts)):
        for r in range(group_rows):
            src, dst = out_piece(c, 0, r)
            pltpu.make_async_copy(src, dst, out_local.at[c, r]).wait()
            for s in range(1, n_grp):
                ref = landing(c, s, r)
                at = (c, s, r)
                remote(ref, ref, out_send.at[at], out_recv.at[at], pair).wait_recv()
    for copy in sent:
        copy.wait_send()


def chunk_cuts(share):
    pieces = share // ROW_TILE
    count = min(CHUNKS, pieces)
    sizes = [(pieces // count + (c < pieces % count)) * ROW_TILE for c in range(count)]
    return [(sum(sizes[:c]), sizes[c]) for c in range(count)]


def exchange_plan(n_grp, n_col, orbitals, cosine_tiles, sine_tiles, tile_row, tile_col, row_place):
    halves, orbital_count, rows_dev = orbitals.shape
    tile_size = cosine_tiles.shape[-1]
    group_rows = rows_dev // tile_size
    slots = tile_row.shape[0]
    blocks = row_place.shape[0]
    n_z = n_col // 2
    cuts = chunk_cuts(orbital_count // n_grp)
    tallest = halves * max(length for _, length in cuts)
    lists = slot_lists(tile_row, tile_col, row_place, group_rows)
    dma = pltpu.SemaphoreType.DMA
    grid = (len(cuts), n_grp, group_rows)
    scratch = [
        pltpu.VMEM((blocks, halves, length, tile_size), orbitals.dtype) for _, length in cuts
    ]
    scratch += [
        pltpu.VMEM((blocks, tallest, tile_size), jnp.bfloat16),
        pltpu.VMEM((slots, tallest, tile_size), jnp.float32),
        pltpu.VMEM((n_grp, slots, tile_size, tile_size), cosine_tiles.dtype),
        pltpu.VMEM((n_grp, slots, tile_size, tile_size), sine_tiles.dtype),
        pltpu.VMEM((n_grp,) + lists.shape, jnp.int32),
        pltpu.SMEM((n_grp,) + lists.shape, jnp.int32),
        dma((n_grp,)),
        dma((n_grp,)),
        dma((1,)),
        dma((2, n_grp, n_z)),
        dma((2, n_grp, n_z)),
        dma((2, n_grp, n_z)),
        dma((2, n_grp, n_z)),
        dma((3,)),
        dma(grid),
        dma(grid),
        dma((len(cuts), group_rows)),
        dma(grid),
        dma(grid),
        dma((len(cuts), group_rows)),
    ]
    return pl.pallas_call(
        functools.partial(kernel, n_grp, n_z, cuts, group_rows),
        out_shape=jax.ShapeDtypeStruct(orbitals.shape, orbitals.dtype),
        in_specs=[pl.BlockSpec(memory_space=pl.ANY)] * 4,
        out_specs=pl.BlockSpec(memory_space=pl.ANY),
        scratch_shapes=scratch,
        compiler_params=pltpu.CompilerParams(
            collective_id=0, has_side_effects=True, vmem_limit_bytes=VMEM_LIMIT
        ),
    )(orbitals, cosine_tiles, sine_tiles, lists)


def on_device(n_grp, n_col, orbitals, cosine_tiles, *rest):
    halves, orbital_count, rows_dev = orbitals.shape
    tile_size = cosine_tiles.shape[-1]
    slots = rest[1].shape[0]
    tile_bytes = 2 * n_grp * slots * tile_size * tile_size * 2
    fits = tile_bytes + 4 * orbitals.size * 2 < VMEM_LIMIT
    even = orbital_count % (n_grp * ROW_TILE) == 0 and tile_size % 128 == 0
    paired = n_col % 2 == 0 and slots == n_col and slots <= 128
    if fits and even and paired and n_grp > 1 and n_col > 2:
        return exchange_plan(n_grp, n_col, orbitals, cosine_tiles, *rest)
    return gather_plan(orbitals, cosine_tiles, *rest)


def solution(mesh):
    in_specs = (
        P(None, "col", "grp"),
        P(("grp", "col"), None, None),
        P(("grp", "col"), None, None),
        P("grp"),
        P("grp"),
        P(),
    )
    out_specs = P(None, "col", "grp")
    return jax.shard_map(
        functools.partial(on_device, mesh.shape["grp"], mesh.shape["col"]),
        mesh=mesh,
        in_specs=in_specs,
        out_specs=out_specs,
        check_vma=False,
    )
```

```python
import functools

import jax
import jax.numpy as jnp
from jax import lax
from jax.experimental import pallas as pl
from jax.experimental.pallas import tpu as pltpu
from jax.sharding import PartitionSpec as P

STEPS = 2
ROW_TILE = 16
CHUNKS = 3
MESH = pl.DeviceIdType.MESH
VMEM_LIMIT = 48 * 2**20


def row_sums(product, rows_onehot):
    group_rows = rows_onehot.shape[1]
    totals = [
        jnp.sum(product * rows_onehot[:, row_number][None, :, None], axis=1)
        for row_number in range(group_rows)
    ]
    return jnp.stack(totals, axis=1)


def tile_product(panels, tiles, rows_onehot, source):
    chosen = jnp.take(panels, source, axis=1)
    product = jnp.einsum("osj,sij->osi", chosen, tiles, preferred_element_type=jnp.float32)
    return row_sums(product, rows_onehot)


def find_source(tile_col, row_place):
    blocks = jnp.arange(row_place.shape[0], dtype=jnp.int32)
    return jnp.sum(jnp.where(tile_col[:, None] == blocks[None, :], row_place[None, :], 0), axis=1)


def gather_plan(orbitals, cosine_tiles, sine_tiles, tile_row, tile_col, row_place):
    halves, orbital_count, rows_dev = orbitals.shape
    tile_size = cosine_tiles.shape[-1]
    group_rows = rows_dev // tile_size
    slab_blocks = row_place.shape[0]
    columns = halves * orbital_count
    source = find_source(tile_col, row_place)
    rows_onehot = (tile_row[:, None] == jnp.arange(group_rows, dtype=jnp.int32)[None, :]).astype(
        jnp.float32
    )
    current = orbitals
    cosine_all = lax.all_gather(cosine_tiles, "col", axis=0, tiled=True)
    sine_all = lax.all_gather(sine_tiles, "col", axis=0, tiled=True)
    for _ in range(STEPS):
        panels = lax.all_gather(current, "grp", axis=2, tiled=True).reshape(
            columns, slab_blocks, tile_size
        )
        direct = tile_product(panels, cosine_all, rows_onehot, source)
        spread = direct.astype(jnp.bfloat16).reshape(halves, orbital_count, rows_dev)
        spread_all = lax.all_gather(spread, "grp", axis=2, tiled=True).reshape(
            columns, slab_blocks, tile_size
        )
        cosine_part = tile_product(spread_all, cosine_all, rows_onehot, source)
        sine_part = tile_product(spread_all, sine_all, rows_onehot, source)
        previous = current.astype(jnp.float32).reshape(columns, group_rows, tile_size)
        real_new = (
            2.0 * (cosine_part[:orbital_count] + sine_part[orbital_count:])
            - previous[:orbital_count]
        )
        imag_new = (
            2.0 * (cosine_part[orbital_count:] - sine_part[:orbital_count])
            - previous[orbital_count:]
        )
        current = (
            jnp.concatenate([real_new, imag_new], axis=0)
            .astype(jnp.bfloat16)
            .reshape(halves, orbital_count, rows_dev)
        )
    return current


def slot_lists(tile_row, tile_col, row_place, group_rows):
    slots = tile_row.shape[0]
    number = jnp.arange(slots, dtype=jnp.int32)
    row = jnp.where(tile_row < 0, group_rows, tile_row)
    key = row * slots + number
    rank = jnp.sum((key[None, :] < key[:, None]).astype(jnp.int32), axis=1)
    place = (rank[None, :] == number[:, None]).astype(jnp.int32)
    source = find_source(tile_col, row_place)
    order = jnp.sum(place * number[None, :], axis=1)
    sorted_source = jnp.sum(place * source[None, :], axis=1)
    sorted_row = jnp.sum(place * row[None, :], axis=1)
    before = jnp.concatenate([jnp.full((1,), -1, jnp.int32), sorted_row[:-1]])
    keep = (sorted_row == before).astype(jnp.int32)
    rows = jnp.arange(group_rows, dtype=jnp.int32)
    last = jnp.maximum(jnp.sum((row[None, :] <= rows[:, None]).astype(jnp.int32), axis=1) - 1, 0)
    used = jnp.max((row[None, :] == rows[:, None]).astype(jnp.int32), axis=1)
    table = [order, sorted_source, keep, last, used]
    table = [jnp.pad(line, (0, 128 - line.shape[0])) for line in table]
    return jnp.pad(jnp.stack(table), ((0, 8 - len(table)), (0, 0)))


def dot_t(panel, tile):
    return lax.dot_general(
        panel, tile, (((1,), (1,)), ((), ())), preferred_element_type=jnp.float32
    )


def stages(current, spread, sums, cosine, sine, table, group_rows, slots):
    halves, length, tile_size = current.shape[1:]
    height = halves * length

    def slot_values(g, k):
        return table[g, 0, k], table[g, 1, k], table[g, 2, k].astype(jnp.float32)

    def spread_group(g, carry):
        total = None
        for k in range(slots):
            slot, source, keep = slot_values(g, k)
            panel = current[source].reshape(height, tile_size)
            product = dot_t(panel, cosine[g, slot])
            total = product if k == 0 else product + total * keep
            sums[k, :height] = total
        for r in range(group_rows):
            used = table[g, 4, r].astype(jnp.float32)
            spread[g * group_rows + r, :height] = (sums[table[g, 3, r], :height] * used).astype(
                spread.dtype
            )
        return carry

    def double_group(g, carry):
        total = None
        for k in range(slots):
            slot, source, keep = slot_values(g, k)
            panel = spread[source, :height]
            by_cosine = dot_t(panel, cosine[g, slot])
            by_sine = dot_t(panel, sine[g, slot])
            product = jnp.concatenate(
                [by_cosine[:length] + by_sine[length:], by_cosine[length:] - by_sine[:length]],
                axis=0,
            )
            total = product if k == 0 else product + total * keep
            sums[k, :height] = total
        for r in range(group_rows):
            used = table[g, 4, r].astype(jnp.float32)
            block = g * group_rows + r
            previous = current[block].reshape(height, tile_size).astype(jnp.float32)
            new = 2.0 * (sums[table[g, 3, r], :height] * used) - previous
            current[block] = new.astype(current.dtype).reshape(halves, length, tile_size)
        return carry

    return spread_group, double_group


def kernel(n_grp, n_z, cuts, group_rows, orb, cos_in, sin_in, lists, out, *scratch):
    currents = scratch[: len(cuts)]
    (
        spread,
        sums,
        cosine,
        sine,
        table_v,
        table,
        list_send,
        list_recv,
        table_sem,
        lane_send,
        lane_recv,
        pair_send,
        pair_recv,
        own_sem,
        in_send,
        in_recv,
        in_local,
        out_send,
        out_recv,
        out_local,
    ) = scratch[len(cuts) :]
    tile_size = cosine.shape[-1]
    slots = cosine.shape[1]
    share = orb.shape[1] // n_grp
    grp, col = lax.axis_index("grp"), lax.axis_index("col")
    z, core = col // 2, col % 2
    tiles = (cosine, sine)
    own = (cos_in.at[0], sin_in.at[0])

    def grp_at(diff):
        return lax.rem(grp // 2 + diff // 2, 2) * 2 + lax.rem(grp + diff, 2)

    def z_at(shift):
        return lax.rem(z + shift + n_z, n_z)

    def device(dg, dz):
        return (grp_at(dg), z_at(dz) * 2 + core)

    pair = (grp, z * 2 + 1 - core)
    sent = []

    def remote(src, dst, send_sem, recv_sem, to):
        return pltpu.make_async_remote_copy(
            src_ref=src,
            dst_ref=dst,
            send_sem=send_sem,
            recv_sem=recv_sem,
            device_id=to,
            device_id_type=MESH,
        )

    def start(copy):
        copy.start()
        sent.append(copy)

    barrier = pltpu.get_barrier_semaphore()
    partners = [device(s, 0) for s in range(1, n_grp)]
    partners += [device(0, s) for s in range(1, n_z)] + [pair]
    for partner in partners:
        pl.semaphore_signal(barrier, inc=1, device_id=partner, device_id_type=MESH)
    pl.semaphore_wait(barrier, len(partners))

    def tile_ref(k, tg, tz, lane):
        return tiles[k].at[grp_at(tg), z_at(-tz) * 2 + lane]

    def lane_copy(k, tg, tz, dg, dz):
        dst = tile_ref(k, tg, tz, core)
        src = own[k] if (tg, tz) == (0, 0) else dst
        at = (k, tg ^ dg, (tz + dz) % n_z)
        return remote(src, dst, lane_send.at[at], lane_recv.at[at], device(dg, dz))

    def lane_wait(k, sg, sz):
        ref = tile_ref(k, sg, sz, core)
        at = (k, sg, sz)
        remote(ref, ref, lane_send.at[at], lane_recv.at[at], pair).wait_recv()

    def pair_copy(k, sg, sz):
        dst = tile_ref(k, sg, sz, core)
        src = own[k] if (sg, sz) == (0, 0) else dst
        at = (k, sg, sz)
        start(remote(src, dst, pair_send.at[at], pair_recv.at[at], pair))

    def pair_wait(k, sg, sz):
        ref = tile_ref(k, sg, sz, 1 - core)
        at = (k, sg, sz)
        remote(ref, ref, pair_send.at[at], pair_recv.at[at], pair).wait_recv()

    guarded = []

    def start_if(condition, copy):
        guarded.append((condition, copy))
        pl.when(condition)(copy.start)

    def pass_on(sg, sz):
        below = z >= sz
        up, down = z < n_z - 1, z > 0
        if sz:
            up, down = jnp.logical_and(up, below), jnp.logical_and(down, jnp.logical_not(below))
        start_if(up, lane_copy(1, sg, sz, 0, 1))
        start_if(down, lane_copy(1, sg, sz, 0, -1))

    others = range(1, n_grp)
    for s in others:
        start(remote(lists, table_v.at[grp], list_send.at[s], list_recv.at[s], device(s, 0)))
    for s in others:
        start(lane_copy(1, 0, 0, s, 0))
    for s in range(1, n_z):
        start(lane_copy(0, 0, 0, 0, s))
    pass_on(0, 0)
    local = [pltpu.make_async_copy(lists, table_v.at[grp], own_sem.at[2])]
    for k in range(2):
        local.append(pltpu.make_async_copy(own[k], tile_ref(k, 0, 0, core), own_sem.at[k]))
    for copy in local:
        copy.start()
    for k in range(2):
        pair_copy(k, 0, 0)
    for s in (1, 2):
        start(lane_copy(0, 0, 0, s, 0))

    def in_piece(c, s, r):
        begin, length = cuts[c]
        rows = pl.ds(pl.multiple_of(grp_at(s) * share + begin, ROW_TILE), length)
        src = orb.at[:, rows, pl.ds(r * tile_size, tile_size)]
        return src, currents[c].at[grp * group_rows + r]

    def send_orbitals(c):
        for r in range(group_rows):
            src, dst = in_piece(c, 0, r)
            pltpu.make_async_copy(src, dst, in_local.at[c, r]).start()
            for s in (3, 1, 2):
                src, dst = in_piece(c, s, r)
                at = (c, s, r)
                start(remote(src, dst, in_send.at[at], in_recv.at[at], device(s, 0)))

    send_orbitals(0)

    near = sorted(range(1, n_z), key=lambda s: (min(s, n_z - s), s))
    for i in range(max(n_grp, n_z) - 1):
        if i < n_z - 1:
            lane_wait(0, 0, near[i])
            for d in (1, 2):
                start(lane_copy(0, 0, near[i], d, 0))
            pair_copy(0, 0, near[i])
        if i < n_grp - 1:
            lane_wait(1, i + 1, 0)
            pass_on(i + 1, 0)
            pair_copy(1, i + 1, 0)
    for c in range(1, len(cuts)):
        send_orbitals(c)

    for sz in [0] + near:
        for d in (1, 2):
            lane_wait(0, d, sz)
            if d == 1 + sz % 2:
                start(lane_copy(0, d, sz, 3 - d, 0))
            pair_copy(0, d, sz)
        if sz:
            for sg in range(n_grp):
                lane_wait(1, sg, sz)
                pass_on(sg, sz)
                pair_copy(1, sg, sz)
    for sz in [0] + near:
        lane_wait(0, 3, sz)
        pair_copy(0, 3, sz)
    for copy in local:
        copy.wait()
    for s in others:
        ref = table_v.at[grp_at(s)]
        remote(ref, ref, list_send.at[s], list_recv.at[s], pair).wait_recv()
    to_scalar = pltpu.make_async_copy(table_v, table, table_sem.at[0])
    to_scalar.start()
    to_scalar.wait()

    def pair_waits(k):
        for sg in range(n_grp):
            for sz in range(n_z):
                pair_wait(k, sg, sz)

    def out_piece(c, s, r):
        begin, length = cuts[c]
        rows = pl.ds(pl.multiple_of(grp * share + begin, ROW_TILE), length)
        dst = out.at[:, rows, pl.ds(r * tile_size, tile_size)]
        return currents[c].at[grp_at(s) * group_rows + r], dst

    def landing(c, s, r):
        begin, length = cuts[c]
        rows = pl.ds(pl.multiple_of(grp_at(s) * share + begin, ROW_TILE), length)
        return out.at[:, rows, pl.ds(r * tile_size, tile_size)]

    for c in range(len(cuts)):
        for r in range(group_rows):
            src, dst = in_piece(c, 0, r)
            pltpu.make_async_copy(src, dst, in_local.at[c, r]).wait()
            for s in range(1, n_grp):
                ref = currents[c].at[grp_at(s) * group_rows + r]
                at = (c, s, r)
                remote(ref, ref, in_send.at[at], in_recv.at[at], pair).wait_recv()
        spread_group, double_group = stages(
            currents[c], spread, sums, cosine, sine, table, group_rows, slots
        )
        if c == 0:
            pair_waits(0)
        lax.fori_loop(0, n_grp, spread_group, 0)
        if c == 0:
            pair_waits(1)

        def step(_, carry):
            lax.fori_loop(0, n_grp, double_group, 0)
            lax.fori_loop(0, n_grp, spread_group, 0)
            return carry

        lax.fori_loop(0, STEPS - 1, step, 0)
        for s in (3, 1, 2, 0):
            double_group(grp_at(s), 0)
            for r in range(group_rows):
                src, dst = out_piece(c, s, r)
                if s == 0:
                    pltpu.make_async_copy(src, dst, out_local.at[c, r]).start()
                else:
                    at = (c, s, r)
                    start(remote(src, dst, out_send.at[at], out_recv.at[at], device(s, 0)))
    for c in range(len(cuts)):
        for r in range(group_rows):
            src, dst = out_piece(c, 0, r)
            pltpu.make_async_copy(src, dst, out_local.at[c, r]).wait()
            for s in range(1, n_grp):
                ref = landing(c, s, r)
                at = (c, s, r)
                remote(ref, ref, out_send.at[at], out_recv.at[at], pair).wait_recv()
    for copy in sent:
        copy.wait_send()
    for condition, copy in guarded:
        pl.when(condition)(copy.wait_send)


def chunk_cuts(share):
    pieces = share // ROW_TILE
    count = min(CHUNKS, pieces)
    sizes = [(pieces // count + (c < pieces % count)) * ROW_TILE for c in range(count)]
    return [(sum(sizes[:c]), sizes[c]) for c in range(count)]


def exchange_plan(n_grp, n_col, orbitals, cosine_tiles, sine_tiles, tile_row, tile_col, row_place):
    halves, orbital_count, rows_dev = orbitals.shape
    tile_size = cosine_tiles.shape[-1]
    group_rows = rows_dev // tile_size
    slots = tile_row.shape[0]
    blocks = row_place.shape[0]
    n_z = n_col // 2
    cuts = chunk_cuts(orbital_count // n_grp)
    tallest = halves * max(length for _, length in cuts)
    lists = slot_lists(tile_row, tile_col, row_place, group_rows)
    dma = pltpu.SemaphoreType.DMA
    grid = (len(cuts), n_grp, group_rows)
    scratch = [
        pltpu.VMEM((blocks, halves, length, tile_size), orbitals.dtype) for _, length in cuts
    ]
    scratch += [
        pltpu.VMEM((blocks, tallest, tile_size), jnp.bfloat16),
        pltpu.VMEM((slots, tallest, tile_size), jnp.float32),
        pltpu.VMEM((n_grp, slots, tile_size, tile_size), cosine_tiles.dtype),
        pltpu.VMEM((n_grp, slots, tile_size, tile_size), sine_tiles.dtype),
        pltpu.VMEM((n_grp,) + lists.shape, jnp.int32),
        pltpu.SMEM((n_grp,) + lists.shape, jnp.int32),
        dma((n_grp,)),
        dma((n_grp,)),
        dma((1,)),
        dma((2, n_grp, n_z)),
        dma((2, n_grp, n_z)),
        dma((2, n_grp, n_z)),
        dma((2, n_grp, n_z)),
        dma((3,)),
        dma(grid),
        dma(grid),
        dma((len(cuts), group_rows)),
        dma(grid),
        dma(grid),
        dma((len(cuts), group_rows)),
    ]
    return pl.pallas_call(
        functools.partial(kernel, n_grp, n_z, cuts, group_rows),
        out_shape=jax.ShapeDtypeStruct(orbitals.shape, orbitals.dtype),
        in_specs=[pl.BlockSpec(memory_space=pltpu.HBM)] * 4,
        out_specs=pl.BlockSpec(memory_space=pl.ANY),
        scratch_shapes=scratch,
        compiler_params=pltpu.CompilerParams(
            collective_id=0, has_side_effects=True, vmem_limit_bytes=VMEM_LIMIT
        ),
    )(orbitals, cosine_tiles, sine_tiles, lists)


def on_device(n_grp, n_col, orbitals, cosine_tiles, *rest):
    halves, orbital_count, rows_dev = orbitals.shape
    tile_size = cosine_tiles.shape[-1]
    slots = rest[1].shape[0]
    tile_bytes = 2 * n_grp * slots * tile_size * tile_size * 2
    fits = tile_bytes + 4 * orbitals.size * 2 < VMEM_LIMIT
    even = orbital_count % (n_grp * ROW_TILE) == 0 and tile_size % 128 == 0
    paired = n_col % 2 == 0 and slots == n_col and slots <= 128
    if fits and even and paired and n_grp == 4 and n_col > 2:
        return exchange_plan(n_grp, n_col, orbitals, cosine_tiles, *rest)
    return gather_plan(orbitals, cosine_tiles, *rest)


def solution(mesh):
    in_specs = (
        P(None, "col", "grp"),
        P(("grp", "col"), None, None),
        P(("grp", "col"), None, None),
        P("grp"),
        P("grp"),
        P(),
    )
    out_specs = P(None, "col", "grp")
    return jax.shard_map(
        functools.partial(on_device, mesh.shape["grp"], mesh.shape["col"]),
        mesh=mesh,
        in_specs=in_specs,
        out_specs=out_specs,
        check_vma=False,
    )
```

```python
import functools

import jax
import jax.numpy as jnp
from jax import lax
from jax.experimental import pallas as pl
from jax.experimental.pallas import tpu as pltpu
from jax.sharding import PartitionSpec as P

STEPS = 2
ROW_TILE = 16
CHUNKS = 3
MESH = pl.DeviceIdType.MESH
VMEM_LIMIT = 48 * 2**20


def row_sums(product, rows_onehot):
    group_rows = rows_onehot.shape[1]
    totals = [
        jnp.sum(product * rows_onehot[:, row_number][None, :, None], axis=1)
        for row_number in range(group_rows)
    ]
    return jnp.stack(totals, axis=1)


def tile_product(panels, tiles, rows_onehot, source):
    chosen = jnp.take(panels, source, axis=1)
    product = jnp.einsum("osj,sij->osi", chosen, tiles, preferred_element_type=jnp.float32)
    return row_sums(product, rows_onehot)


def find_source(tile_col, row_place):
    blocks = jnp.arange(row_place.shape[0], dtype=jnp.int32)
    return jnp.sum(jnp.where(tile_col[:, None] == blocks[None, :], row_place[None, :], 0), axis=1)


def gather_plan(orbitals, cosine_tiles, sine_tiles, tile_row, tile_col, row_place):
    halves, orbital_count, rows_dev = orbitals.shape
    tile_size = cosine_tiles.shape[-1]
    group_rows = rows_dev // tile_size
    slab_blocks = row_place.shape[0]
    columns = halves * orbital_count
    source = find_source(tile_col, row_place)
    rows_onehot = (tile_row[:, None] == jnp.arange(group_rows, dtype=jnp.int32)[None, :]).astype(
        jnp.float32
    )
    current = orbitals
    cosine_all = lax.all_gather(cosine_tiles, "col", axis=0, tiled=True)
    sine_all = lax.all_gather(sine_tiles, "col", axis=0, tiled=True)
    for _ in range(STEPS):
        panels = lax.all_gather(current, "grp", axis=2, tiled=True).reshape(
            columns, slab_blocks, tile_size
        )
        direct = tile_product(panels, cosine_all, rows_onehot, source)
        spread = direct.astype(jnp.bfloat16).reshape(halves, orbital_count, rows_dev)
        spread_all = lax.all_gather(spread, "grp", axis=2, tiled=True).reshape(
            columns, slab_blocks, tile_size
        )
        cosine_part = tile_product(spread_all, cosine_all, rows_onehot, source)
        sine_part = tile_product(spread_all, sine_all, rows_onehot, source)
        previous = current.astype(jnp.float32).reshape(columns, group_rows, tile_size)
        real_new = (
            2.0 * (cosine_part[:orbital_count] + sine_part[orbital_count:])
            - previous[:orbital_count]
        )
        imag_new = (
            2.0 * (cosine_part[orbital_count:] - sine_part[:orbital_count])
            - previous[orbital_count:]
        )
        current = (
            jnp.concatenate([real_new, imag_new], axis=0)
            .astype(jnp.bfloat16)
            .reshape(halves, orbital_count, rows_dev)
        )
    return current


def slot_lists(tile_row, tile_col, row_place, group_rows):
    slots = tile_row.shape[0]
    number = jnp.arange(slots, dtype=jnp.int32)
    row = jnp.where(tile_row < 0, group_rows, tile_row)
    key = row * slots + number
    rank = jnp.sum((key[None, :] < key[:, None]).astype(jnp.int32), axis=1)
    place = (rank[None, :] == number[:, None]).astype(jnp.int32)
    source = find_source(tile_col, row_place)
    order = jnp.sum(place * number[None, :], axis=1)
    sorted_source = jnp.sum(place * source[None, :], axis=1)
    sorted_row = jnp.sum(place * row[None, :], axis=1)
    before = jnp.concatenate([jnp.full((1,), -1, jnp.int32), sorted_row[:-1]])
    keep = (sorted_row == before).astype(jnp.int32)
    rows = jnp.arange(group_rows, dtype=jnp.int32)
    last = jnp.maximum(jnp.sum((row[None, :] <= rows[:, None]).astype(jnp.int32), axis=1) - 1, 0)
    used = jnp.max((row[None, :] == rows[:, None]).astype(jnp.int32), axis=1)
    table = [order, sorted_source, keep, last, used]
    table = [jnp.pad(line, (0, 128 - line.shape[0])) for line in table]
    return jnp.pad(jnp.stack(table), ((0, 8 - len(table)), (0, 0)))


def dot(panel, tile):
    return jnp.dot(panel, tile, preferred_element_type=jnp.float32)


def stages(current, spread, sums, cosine, sine, table, group_rows, slots):
    halves, length, tile_size = current.shape[1:]
    height = halves * length

    def slot_values(g, k):
        return table[g, 0, k], table[g, 1, k], table[g, 2, k].astype(jnp.float32)

    def spread_group(g, carry):
        total = None
        for k in range(slots):
            slot, source, keep = slot_values(g, k)
            panel = current[source].reshape(height, tile_size)
            product = dot(panel, cosine[g, slot])
            total = product if k == 0 else product + total * keep
            sums[k, :height] = total
        for r in range(group_rows):
            used = table[g, 4, r].astype(jnp.float32)
            spread[g * group_rows + r, :height] = (sums[table[g, 3, r], :height] * used).astype(
                spread.dtype
            )
        return carry

    def double_group(g, carry):
        total = None
        for k in range(slots):
            slot, source, keep = slot_values(g, k)
            panel = spread[source, :height]
            by_cosine = dot(panel, cosine[g, slot])
            by_sine = dot(panel, sine[g, slot])
            product = jnp.concatenate(
                [by_cosine[:length] + by_sine[length:], by_cosine[length:] - by_sine[:length]],
                axis=0,
            )
            total = product if k == 0 else product + total * keep
            sums[k, :height] = total
        for r in range(group_rows):
            used = table[g, 4, r].astype(jnp.float32)
            block = g * group_rows + r
            previous = current[block].reshape(height, tile_size).astype(jnp.float32)
            new = 2.0 * (sums[table[g, 3, r], :height] * used) - previous
            current[block] = new.astype(current.dtype).reshape(halves, length, tile_size)
        return carry

    return spread_group, double_group


def kernel(n_grp, n_z, cuts, group_rows, orb, cos_in, sin_in, lists, out, *scratch):
    currents = scratch[: len(cuts)]
    (
        spread,
        sums,
        cosine,
        sine,
        table_v,
        table,
        list_send,
        list_recv,
        table_sem,
        lane_send,
        lane_recv,
        pair_send,
        pair_recv,
        own_sem,
        in_send,
        in_recv,
        in_local,
        out_send,
        out_recv,
        out_local,
    ) = scratch[len(cuts) :]
    tile_size = cosine.shape[-1]
    slots = cosine.shape[1]
    share = orb.shape[1] // n_grp
    grp, col = lax.axis_index("grp"), lax.axis_index("col")
    z, core = col // 2, col % 2
    tiles = (cosine, sine)
    own = (cos_in.at[0], sin_in.at[0])

    def grp_at(diff):
        return lax.rem(grp // 2 + diff // 2, 2) * 2 + lax.rem(grp + diff, 2)

    def z_at(shift):
        return lax.rem(z + shift + n_z, n_z)

    def device(dg, dz):
        return (grp_at(dg), z_at(dz) * 2 + core)

    pair = (grp, z * 2 + 1 - core)
    sent = []

    def remote(src, dst, send_sem, recv_sem, to):
        return pltpu.make_async_remote_copy(
            src_ref=src,
            dst_ref=dst,
            send_sem=send_sem,
            recv_sem=recv_sem,
            device_id=to,
            device_id_type=MESH,
        )

    def start(copy):
        copy.start()
        sent.append(copy)

    barrier = pltpu.get_barrier_semaphore()
    partners = [device(s, 0) for s in range(1, n_grp)]
    partners += [device(0, s) for s in range(1, n_z)] + [pair]
    for partner in partners:
        pl.semaphore_signal(barrier, inc=1, device_id=partner, device_id_type=MESH)
    pl.semaphore_wait(barrier, len(partners))

    def tile_ref(k, tg, tz, lane):
        return tiles[k].at[grp_at(tg), z_at(-tz) * 2 + lane]

    def lane_copy(k, tg, tz, dg, dz):
        dst = tile_ref(k, tg, tz, core)
        src = own[k] if (tg, tz) == (0, 0) else dst
        at = (k, tg ^ dg, (tz + dz) % n_z)
        return remote(src, dst, lane_send.at[at], lane_recv.at[at], device(dg, dz))

    def lane_wait(k, sg, sz):
        ref = tile_ref(k, sg, sz, core)
        at = (k, sg, sz)
        remote(ref, ref, lane_send.at[at], lane_recv.at[at], pair).wait_recv()

    def pair_copy(k, sg, sz):
        dst = tile_ref(k, sg, sz, core)
        src = own[k] if (sg, sz) == (0, 0) else dst
        at = (k, sg, sz)
        start(remote(src, dst, pair_send.at[at], pair_recv.at[at], pair))

    def pair_wait(k, sg, sz):
        ref = tile_ref(k, sg, sz, 1 - core)
        at = (k, sg, sz)
        remote(ref, ref, pair_send.at[at], pair_recv.at[at], pair).wait_recv()

    guarded = []

    def start_if(condition, copy):
        guarded.append((condition, copy))
        pl.when(condition)(copy.start)

    def pass_on(sg, sz):
        below = z >= sz
        up, down = z < n_z - 1, z > 0
        if sz:
            up, down = jnp.logical_and(up, below), jnp.logical_and(down, jnp.logical_not(below))
        start_if(up, lane_copy(1, sg, sz, 0, 1))
        start_if(down, lane_copy(1, sg, sz, 0, -1))

    others = range(1, n_grp)
    for s in others:
        start(remote(lists, table_v.at[grp], list_send.at[s], list_recv.at[s], device(s, 0)))
    for s in others:
        start(lane_copy(1, 0, 0, s, 0))
    for s in range(1, n_z):
        start(lane_copy(0, 0, 0, 0, s))
    pass_on(0, 0)
    local = [pltpu.make_async_copy(lists, table_v.at[grp], own_sem.at[2])]
    for k in range(2):
        local.append(pltpu.make_async_copy(own[k], tile_ref(k, 0, 0, core), own_sem.at[k]))
    for copy in local:
        copy.start()
    for k in range(2):
        pair_copy(k, 0, 0)
    for s in (1, 2):
        start(lane_copy(0, 0, 0, s, 0))

    def in_piece(c, s, r):
        begin, length = cuts[c]
        rows = pl.ds(pl.multiple_of(grp_at(s) * share + begin, ROW_TILE), length)
        src = orb.at[:, rows, pl.ds(r * tile_size, tile_size)]
        return src, currents[c].at[grp * group_rows + r]

    def send_orbitals(c):
        for r in range(group_rows):
            src, dst = in_piece(c, 0, r)
            pltpu.make_async_copy(src, dst, in_local.at[c, r]).start()
            for s in (3, 1, 2):
                src, dst = in_piece(c, s, r)
                at = (c, s, r)
                start(remote(src, dst, in_send.at[at], in_recv.at[at], device(s, 0)))

    send_orbitals(0)

    near = sorted(range(1, n_z), key=lambda s: (min(s, n_z - s), s))
    for i in range(max(n_grp, n_z) - 1):
        if i < n_z - 1:
            lane_wait(0, 0, near[i])
            for d in (1, 2):
                start(lane_copy(0, 0, near[i], d, 0))
            pair_copy(0, 0, near[i])
        if i < n_grp - 1:
            lane_wait(1, i + 1, 0)
            pass_on(i + 1, 0)
            pair_copy(1, i + 1, 0)
    for c in range(1, len(cuts)):
        send_orbitals(c)

    for sz in [0] + near:
        for d in (1, 2):
            lane_wait(0, d, sz)
            if d == 1 + sz % 2:
                start(lane_copy(0, d, sz, 3 - d, 0))
            pair_copy(0, d, sz)
        if sz:
            for sg in range(n_grp):
                lane_wait(1, sg, sz)
                pass_on(sg, sz)
                pair_copy(1, sg, sz)
    for sz in [0] + near:
        lane_wait(0, 3, sz)
        pair_copy(0, 3, sz)
    for copy in local:
        copy.wait()
    for s in others:
        ref = table_v.at[grp_at(s)]
        remote(ref, ref, list_send.at[s], list_recv.at[s], pair).wait_recv()
    to_scalar = pltpu.make_async_copy(table_v, table, table_sem.at[0])
    to_scalar.start()
    to_scalar.wait()

    def pair_waits(k):
        for sg in range(n_grp):
            for sz in range(n_z):
                pair_wait(k, sg, sz)

    def out_piece(c, s, r):
        begin, length = cuts[c]
        rows = pl.ds(pl.multiple_of(grp * share + begin, ROW_TILE), length)
        dst = out.at[:, rows, pl.ds(r * tile_size, tile_size)]
        return currents[c].at[grp_at(s) * group_rows + r], dst

    def landing(c, s, r):
        begin, length = cuts[c]
        rows = pl.ds(pl.multiple_of(grp_at(s) * share + begin, ROW_TILE), length)
        return out.at[:, rows, pl.ds(r * tile_size, tile_size)]

    for c in range(len(cuts)):
        for r in range(group_rows):
            src, dst = in_piece(c, 0, r)
            pltpu.make_async_copy(src, dst, in_local.at[c, r]).wait()
            for s in range(1, n_grp):
                ref = currents[c].at[grp_at(s) * group_rows + r]
                at = (c, s, r)
                remote(ref, ref, in_send.at[at], in_recv.at[at], pair).wait_recv()
        spread_group, double_group = stages(
            currents[c], spread, sums, cosine, sine, table, group_rows, slots
        )
        if c == 0:
            pair_waits(0)
        lax.fori_loop(0, n_grp, spread_group, 0)
        if c == 0:
            pair_waits(1)

        def step(_, carry):
            lax.fori_loop(0, n_grp, double_group, 0)
            lax.fori_loop(0, n_grp, spread_group, 0)
            return carry

        lax.fori_loop(0, STEPS - 1, step, 0)
        for s in (3, 1, 2, 0):
            double_group(grp_at(s), 0)
            for r in range(group_rows):
                src, dst = out_piece(c, s, r)
                if s == 0:
                    pltpu.make_async_copy(src, dst, out_local.at[c, r]).start()
                else:
                    at = (c, s, r)
                    start(remote(src, dst, out_send.at[at], out_recv.at[at], device(s, 0)))
    for c in range(len(cuts)):
        for r in range(group_rows):
            src, dst = out_piece(c, 0, r)
            pltpu.make_async_copy(src, dst, out_local.at[c, r]).wait()
            for s in range(1, n_grp):
                ref = landing(c, s, r)
                at = (c, s, r)
                remote(ref, ref, out_send.at[at], out_recv.at[at], pair).wait_recv()
    for copy in sent:
        copy.wait_send()
    for condition, copy in guarded:
        pl.when(condition)(copy.wait_send)


def chunk_cuts(share):
    pieces = share // ROW_TILE
    count = min(CHUNKS, pieces)
    sizes = [(pieces // count + (c < pieces % count)) * ROW_TILE for c in range(count)]
    return [(sum(sizes[:c]), sizes[c]) for c in range(count)]


def exchange_plan(n_grp, n_col, orbitals, cosine_tiles, sine_tiles, tile_row, tile_col, row_place):
    halves, orbital_count, rows_dev = orbitals.shape
    tile_size = cosine_tiles.shape[-1]
    group_rows = rows_dev // tile_size
    slots = tile_row.shape[0]
    blocks = row_place.shape[0]
    n_z = n_col // 2
    cuts = chunk_cuts(orbital_count // n_grp)
    tallest = halves * max(length for _, length in cuts)
    lists = slot_lists(tile_row, tile_col, row_place, group_rows)
    dma = pltpu.SemaphoreType.DMA
    grid = (len(cuts), n_grp, group_rows)
    scratch = [
        pltpu.VMEM((blocks, halves, length, tile_size), orbitals.dtype) for _, length in cuts
    ]
    scratch += [
        pltpu.VMEM((blocks, tallest, tile_size), jnp.bfloat16),
        pltpu.VMEM((slots, tallest, tile_size), jnp.float32),
        pltpu.VMEM((n_grp, slots, tile_size, tile_size), cosine_tiles.dtype),
        pltpu.VMEM((n_grp, slots, tile_size, tile_size), sine_tiles.dtype),
        pltpu.VMEM((n_grp,) + lists.shape, jnp.int32),
        pltpu.SMEM((n_grp,) + lists.shape, jnp.int32),
        dma((n_grp,)),
        dma((n_grp,)),
        dma((1,)),
        dma((2, n_grp, n_z)),
        dma((2, n_grp, n_z)),
        dma((2, n_grp, n_z)),
        dma((2, n_grp, n_z)),
        dma((3,)),
        dma(grid),
        dma(grid),
        dma((len(cuts), group_rows)),
        dma(grid),
        dma(grid),
        dma((len(cuts), group_rows)),
    ]
    return pl.pallas_call(
        functools.partial(kernel, n_grp, n_z, cuts, group_rows),
        out_shape=jax.ShapeDtypeStruct(orbitals.shape, orbitals.dtype),
        in_specs=[pl.BlockSpec(memory_space=pltpu.HBM)] * 4,
        out_specs=pl.BlockSpec(memory_space=pl.ANY),
        scratch_shapes=scratch,
        compiler_params=pltpu.CompilerParams(
            collective_id=0, has_side_effects=True, vmem_limit_bytes=VMEM_LIMIT
        ),
    )(orbitals, jnp.swapaxes(cosine_tiles, 1, 2), jnp.swapaxes(sine_tiles, 1, 2), lists)


def on_device(n_grp, n_col, orbitals, cosine_tiles, *rest):
    halves, orbital_count, rows_dev = orbitals.shape
    tile_size = cosine_tiles.shape[-1]
    slots = rest[1].shape[0]
    tile_bytes = 2 * n_grp * slots * tile_size * tile_size * 2
    fits = tile_bytes + 4 * orbitals.size * 2 < VMEM_LIMIT
    even = orbital_count % (n_grp * ROW_TILE) == 0 and tile_size % 128 == 0
    paired = n_col % 2 == 0 and slots == n_col and slots <= 128
    if fits and even and paired and n_grp == 4 and n_col > 2:
        return exchange_plan(n_grp, n_col, orbitals, cosine_tiles, *rest)
    return gather_plan(orbitals, cosine_tiles, *rest)


def solution(mesh):
    in_specs = (
        P(None, "col", "grp"),
        P(("grp", "col"), None, None),
        P(("grp", "col"), None, None),
        P("grp"),
        P("grp"),
        P(),
    )
    out_specs = P(None, "col", "grp")
    return jax.shard_map(
        functools.partial(on_device, mesh.shape["grp"], mesh.shape["col"]),
        mesh=mesh,
        in_specs=in_specs,
        out_specs=out_specs,
        check_vma=False,
    )
```

```python
import functools

import jax
import jax.numpy as jnp
from jax import lax
from jax.experimental import pallas as pl
from jax.experimental.pallas import tpu as pltpu
from jax.sharding import PartitionSpec as P

STEPS = 2
ROW_TILE = 16
CHUNKS = 3
MESH = pl.DeviceIdType.MESH
VMEM_LIMIT = 48 * 2**20


def row_sums(product, rows_onehot):
    group_rows = rows_onehot.shape[1]
    totals = [
        jnp.sum(product * rows_onehot[:, row_number][None, :, None], axis=1)
        for row_number in range(group_rows)
    ]
    return jnp.stack(totals, axis=1)


def tile_product(panels, tiles, rows_onehot, source):
    chosen = jnp.take(panels, source, axis=1)
    product = jnp.einsum("osj,sij->osi", chosen, tiles, preferred_element_type=jnp.float32)
    return row_sums(product, rows_onehot)


def find_source(tile_col, row_place):
    blocks = jnp.arange(row_place.shape[0], dtype=jnp.int32)
    return jnp.sum(jnp.where(tile_col[:, None] == blocks[None, :], row_place[None, :], 0), axis=1)


def gather_plan(orbitals, cosine_tiles, sine_tiles, tile_row, tile_col, row_place):
    halves, orbital_count, rows_dev = orbitals.shape
    tile_size = cosine_tiles.shape[-1]
    group_rows = rows_dev // tile_size
    slab_blocks = row_place.shape[0]
    columns = halves * orbital_count
    source = find_source(tile_col, row_place)
    rows_onehot = (tile_row[:, None] == jnp.arange(group_rows, dtype=jnp.int32)[None, :]).astype(
        jnp.float32
    )
    current = orbitals
    cosine_all = lax.all_gather(cosine_tiles, "col", axis=0, tiled=True)
    sine_all = lax.all_gather(sine_tiles, "col", axis=0, tiled=True)
    for _ in range(STEPS):
        panels = lax.all_gather(current, "grp", axis=2, tiled=True).reshape(
            columns, slab_blocks, tile_size
        )
        direct = tile_product(panels, cosine_all, rows_onehot, source)
        spread = direct.astype(jnp.bfloat16).reshape(halves, orbital_count, rows_dev)
        spread_all = lax.all_gather(spread, "grp", axis=2, tiled=True).reshape(
            columns, slab_blocks, tile_size
        )
        cosine_part = tile_product(spread_all, cosine_all, rows_onehot, source)
        sine_part = tile_product(spread_all, sine_all, rows_onehot, source)
        previous = current.astype(jnp.float32).reshape(columns, group_rows, tile_size)
        real_new = (
            2.0 * (cosine_part[:orbital_count] + sine_part[orbital_count:])
            - previous[:orbital_count]
        )
        imag_new = (
            2.0 * (cosine_part[orbital_count:] - sine_part[:orbital_count])
            - previous[orbital_count:]
        )
        current = (
            jnp.concatenate([real_new, imag_new], axis=0)
            .astype(jnp.bfloat16)
            .reshape(halves, orbital_count, rows_dev)
        )
    return current


def slot_lists(tile_row, tile_col, row_place, group_rows):
    slots = tile_row.shape[0]
    number = jnp.arange(slots, dtype=jnp.int32)
    row = jnp.where(tile_row < 0, group_rows, tile_row)
    key = row * slots + number
    rank = jnp.sum((key[None, :] < key[:, None]).astype(jnp.int32), axis=1)
    place = (rank[None, :] == number[:, None]).astype(jnp.int32)
    source = find_source(tile_col, row_place)
    order = jnp.sum(place * number[None, :], axis=1)
    sorted_source = jnp.sum(place * source[None, :], axis=1)
    sorted_row = jnp.sum(place * row[None, :], axis=1)
    before = jnp.concatenate([jnp.full((1,), -1, jnp.int32), sorted_row[:-1]])
    keep = (sorted_row == before).astype(jnp.int32)
    rows = jnp.arange(group_rows, dtype=jnp.int32)
    last = jnp.maximum(jnp.sum((row[None, :] <= rows[:, None]).astype(jnp.int32), axis=1) - 1, 0)
    used = jnp.max((row[None, :] == rows[:, None]).astype(jnp.int32), axis=1)
    table = [order, sorted_source, keep, last, used]
    table = [jnp.pad(line, (0, 128 - line.shape[0])) for line in table]
    return jnp.pad(jnp.stack(table), ((0, 8 - len(table)), (0, 0)))


def dot(panel, tile):
    return jnp.dot(panel, tile, preferred_element_type=jnp.float32)


def stages(current, spread, sums, cosine, sine, table, group_rows, slots):
    halves, length, tile_size = current.shape[1:]
    height = halves * length

    def slot_values(g, k):
        return table[g, 0, k], table[g, 1, k], table[g, 2, k].astype(jnp.float32)

    def spread_group(g, carry):
        total = None
        for k in range(slots):
            slot, source, keep = slot_values(g, k)
            panel = current[source].reshape(height, tile_size)
            product = dot(panel, cosine[g, slot])
            total = product if k == 0 else product + total * keep
            sums[k, :height] = total
        for r in range(group_rows):
            used = table[g, 4, r].astype(jnp.float32)
            spread[g * group_rows + r, :height] = (sums[table[g, 3, r], :height] * used).astype(
                spread.dtype
            )
        return carry

    def double_group(g, carry):
        total = None
        for k in range(slots):
            slot, source, keep = slot_values(g, k)
            panel = spread[source, :height]
            by_cosine = dot(panel, cosine[g, slot])
            by_sine = dot(panel, sine[g, slot])
            product = jnp.concatenate(
                [by_cosine[:length] + by_sine[length:], by_cosine[length:] - by_sine[:length]],
                axis=0,
            )
            total = product if k == 0 else product + total * keep
            sums[k, :height] = total
        for r in range(group_rows):
            used = table[g, 4, r].astype(jnp.float32)
            block = g * group_rows + r
            previous = current[block].reshape(height, tile_size).astype(jnp.float32)
            new = 2.0 * (sums[table[g, 3, r], :height] * used) - previous
            current[block] = new.astype(current.dtype).reshape(halves, length, tile_size)
        return carry

    return spread_group, double_group


def kernel(n_grp, n_z, cuts, group_rows, orb, cos_in, sin_in, lists, out, *scratch):
    currents = scratch[: len(cuts)]
    (
        spread,
        sums,
        cosine,
        sine,
        table_v,
        table,
        list_send,
        list_recv,
        table_sem,
        lane_send,
        lane_recv,
        pair_send,
        pair_recv,
        own_sem,
        in_send,
        in_recv,
        in_local,
        out_send,
        out_recv,
        out_local,
    ) = scratch[len(cuts) :]
    tile_size = cosine.shape[-1]
    slots = cosine.shape[1]
    share = orb.shape[1] // n_grp
    grp, col = lax.axis_index("grp"), lax.axis_index("col")
    z, core = col // 2, col % 2
    tiles = (cosine, sine)

    def grp_at(diff):
        return lax.rem(grp // 2 + diff // 2, 2) * 2 + lax.rem(grp + diff, 2)

    def z_at(shift):
        return lax.rem(z + shift + n_z, n_z)

    def device(dg, dz):
        return (grp_at(dg), z_at(dz) * 2 + core)

    pair = (grp, z * 2 + 1 - core)
    sent = []

    def remote(src, dst, send_sem, recv_sem, to):
        return pltpu.make_async_remote_copy(
            src_ref=src,
            dst_ref=dst,
            send_sem=send_sem,
            recv_sem=recv_sem,
            device_id=to,
            device_id_type=MESH,
        )

    def start(copy):
        copy.start()
        sent.append(copy)

    barrier = pltpu.get_barrier_semaphore()
    partners = [device(s, 0) for s in range(1, n_grp)]
    partners += [device(0, s) for s in range(1, n_z)] + [pair]
    for partner in partners:
        pl.semaphore_signal(barrier, inc=1, device_id=partner, device_id_type=MESH)
    cosine[grp, col] = cos_in[0].T
    sine[grp, col] = sin_in[0].T
    pl.semaphore_wait(barrier, len(partners))

    def tile_ref(k, tg, tz, lane):
        return tiles[k].at[grp_at(tg), z_at(-tz) * 2 + lane]

    def lane_copy(k, tg, tz, dg, dz):
        dst = tile_ref(k, tg, tz, core)
        at = (k, tg ^ dg, (tz + dz) % n_z)
        return remote(dst, dst, lane_send.at[at], lane_recv.at[at], device(dg, dz))

    def lane_wait(k, sg, sz):
        ref = tile_ref(k, sg, sz, core)
        at = (k, sg, sz)
        remote(ref, ref, lane_send.at[at], lane_recv.at[at], pair).wait_recv()

    def pair_copy(k, sg, sz):
        dst = tile_ref(k, sg, sz, core)
        at = (k, sg, sz)
        start(remote(dst, dst, pair_send.at[at], pair_recv.at[at], pair))

    def pair_wait(k, sg, sz):
        ref = tile_ref(k, sg, sz, 1 - core)
        at = (k, sg, sz)
        remote(ref, ref, pair_send.at[at], pair_recv.at[at], pair).wait_recv()

    guarded = []

    def start_if(condition, copy):
        guarded.append((condition, copy))
        pl.when(condition)(copy.start)

    def pass_on(sg, sz):
        below = z >= sz
        up, down = z < n_z - 1, z > 0
        if sz:
            up, down = jnp.logical_and(up, below), jnp.logical_and(down, jnp.logical_not(below))
        start_if(up, lane_copy(1, sg, sz, 0, 1))
        start_if(down, lane_copy(1, sg, sz, 0, -1))

    others = range(1, n_grp)
    for s in others:
        start(remote(lists, table_v.at[grp], list_send.at[s], list_recv.at[s], device(s, 0)))
    for s in others:
        start(lane_copy(1, 0, 0, s, 0))
    for s in range(1, n_z):
        start(lane_copy(0, 0, 0, 0, s))
    pass_on(0, 0)
    own_lists = pltpu.make_async_copy(lists, table_v.at[grp], own_sem.at[0])
    own_lists.start()
    for k in range(2):
        pair_copy(k, 0, 0)
    for s in (1, 2):
        start(lane_copy(0, 0, 0, s, 0))

    def in_piece(c, s, r):
        begin, length = cuts[c]
        rows = pl.ds(pl.multiple_of(grp_at(s) * share + begin, ROW_TILE), length)
        src = orb.at[:, rows, pl.ds(r * tile_size, tile_size)]
        return src, currents[c].at[grp * group_rows + r]

    def send_orbitals(c):
        for r in range(group_rows):
            src, dst = in_piece(c, 0, r)
            pltpu.make_async_copy(src, dst, in_local.at[c, r]).start()
            for s in (3, 1, 2):
                src, dst = in_piece(c, s, r)
                at = (c, s, r)
                start(remote(src, dst, in_send.at[at], in_recv.at[at], device(s, 0)))

    send_orbitals(0)

    near = sorted(range(1, n_z), key=lambda s: (min(s, n_z - s), s))
    for i in range(max(n_grp, n_z) - 1):
        if i < n_z - 1:
            lane_wait(0, 0, near[i])
            for d in (1, 2):
                start(lane_copy(0, 0, near[i], d, 0))
            pair_copy(0, 0, near[i])
        if i < n_grp - 1:
            lane_wait(1, i + 1, 0)
            pass_on(i + 1, 0)
            pair_copy(1, i + 1, 0)
    def cosine_across(sz):
        for d in (1, 2):
            lane_wait(0, d, sz)
            if d == 1 + sz % 2:
                start(lane_copy(0, d, sz, 3 - d, 0))
            pair_copy(0, d, sz)

    def sine_along(sz):
        for sg in range(n_grp):
            lane_wait(1, sg, sz)
            pass_on(sg, sz)
            pair_copy(1, sg, sz)

    cosine_across(0)
    for sz in near[:2]:
        sine_along(sz)
    for sz in near:
        cosine_across(sz)
    for c in range(1, len(cuts)):
        send_orbitals(c)
    for sz in near[2:]:
        sine_along(sz)
    for sz in [0] + near:
        lane_wait(0, 3, sz)
        pair_copy(0, 3, sz)
    own_lists.wait()
    for s in others:
        ref = table_v.at[grp_at(s)]
        remote(ref, ref, list_send.at[s], list_recv.at[s], pair).wait_recv()
    to_scalar = pltpu.make_async_copy(table_v, table, table_sem.at[0])
    to_scalar.start()
    to_scalar.wait()

    def pair_waits(k):
        for sg in range(n_grp):
            for sz in range(n_z):
                pair_wait(k, sg, sz)

    def out_piece(c, s, r):
        begin, length = cuts[c]
        rows = pl.ds(pl.multiple_of(grp * share + begin, ROW_TILE), length)
        dst = out.at[:, rows, pl.ds(r * tile_size, tile_size)]
        return currents[c].at[grp_at(s) * group_rows + r], dst

    def landing(c, s, r):
        begin, length = cuts[c]
        rows = pl.ds(pl.multiple_of(grp_at(s) * share + begin, ROW_TILE), length)
        return out.at[:, rows, pl.ds(r * tile_size, tile_size)]

    for c in range(len(cuts)):
        for r in range(group_rows):
            src, dst = in_piece(c, 0, r)
            pltpu.make_async_copy(src, dst, in_local.at[c, r]).wait()
            for s in range(1, n_grp):
                ref = currents[c].at[grp_at(s) * group_rows + r]
                at = (c, s, r)
                remote(ref, ref, in_send.at[at], in_recv.at[at], pair).wait_recv()
        spread_group, double_group = stages(
            currents[c], spread, sums, cosine, sine, table, group_rows, slots
        )
        if c == 0:
            pair_waits(0)
        lax.fori_loop(0, n_grp, spread_group, 0)
        if c == 0:
            pair_waits(1)

        def step(_, carry):
            lax.fori_loop(0, n_grp, double_group, 0)
            lax.fori_loop(0, n_grp, spread_group, 0)
            return carry

        lax.fori_loop(0, STEPS - 1, step, 0)
        for s in (3, 1, 2, 0):
            double_group(grp_at(s), 0)
            for r in range(group_rows):
                src, dst = out_piece(c, s, r)
                if s == 0:
                    pltpu.make_async_copy(src, dst, out_local.at[c, r]).start()
                else:
                    at = (c, s, r)
                    start(remote(src, dst, out_send.at[at], out_recv.at[at], device(s, 0)))
    for c in range(len(cuts)):
        for r in range(group_rows):
            src, dst = out_piece(c, 0, r)
            pltpu.make_async_copy(src, dst, out_local.at[c, r]).wait()
            for s in range(1, n_grp):
                ref = landing(c, s, r)
                at = (c, s, r)
                remote(ref, ref, out_send.at[at], out_recv.at[at], pair).wait_recv()
    for copy in sent:
        copy.wait_send()
    for condition, copy in guarded:
        pl.when(condition)(copy.wait_send)


def chunk_cuts(share):
    pieces = share // ROW_TILE
    count = min(CHUNKS, pieces)
    sizes = [(pieces // count + (c < pieces % count)) * ROW_TILE for c in range(count)]
    return [(sum(sizes[:c]), sizes[c]) for c in range(count)]


def exchange_plan(n_grp, n_col, orbitals, cosine_tiles, sine_tiles, tile_row, tile_col, row_place):
    halves, orbital_count, rows_dev = orbitals.shape
    tile_size = cosine_tiles.shape[-1]
    group_rows = rows_dev // tile_size
    slots = tile_row.shape[0]
    blocks = row_place.shape[0]
    n_z = n_col // 2
    cuts = chunk_cuts(orbital_count // n_grp)
    tallest = halves * max(length for _, length in cuts)
    lists = slot_lists(tile_row, tile_col, row_place, group_rows)
    dma = pltpu.SemaphoreType.DMA
    grid = (len(cuts), n_grp, group_rows)
    scratch = [
        pltpu.VMEM((blocks, halves, length, tile_size), orbitals.dtype) for _, length in cuts
    ]
    scratch += [
        pltpu.VMEM((blocks, tallest, tile_size), jnp.bfloat16),
        pltpu.VMEM((slots, tallest, tile_size), jnp.float32),
        pltpu.VMEM((n_grp, slots, tile_size, tile_size), cosine_tiles.dtype),
        pltpu.VMEM((n_grp, slots, tile_size, tile_size), sine_tiles.dtype),
        pltpu.VMEM((n_grp,) + lists.shape, jnp.int32),
        pltpu.SMEM((n_grp,) + lists.shape, jnp.int32),
        dma((n_grp,)),
        dma((n_grp,)),
        dma((1,)),
        dma((2, n_grp, n_z)),
        dma((2, n_grp, n_z)),
        dma((2, n_grp, n_z)),
        dma((2, n_grp, n_z)),
        dma((1,)),
        dma(grid),
        dma(grid),
        dma((len(cuts), group_rows)),
        dma(grid),
        dma(grid),
        dma((len(cuts), group_rows)),
    ]
    return pl.pallas_call(
        functools.partial(kernel, n_grp, n_z, cuts, group_rows),
        out_shape=jax.ShapeDtypeStruct(orbitals.shape, orbitals.dtype),
        in_specs=[pl.BlockSpec(memory_space=space) for space in (pltpu.HBM, pltpu.VMEM, pltpu.VMEM, pltpu.HBM)],
        out_specs=pl.BlockSpec(memory_space=pl.ANY),
        scratch_shapes=scratch,
        compiler_params=pltpu.CompilerParams(
            collective_id=0, has_side_effects=True, vmem_limit_bytes=VMEM_LIMIT
        ),
    )(orbitals, cosine_tiles, sine_tiles, lists)


def on_device(n_grp, n_col, orbitals, cosine_tiles, *rest):
    halves, orbital_count, rows_dev = orbitals.shape
    tile_size = cosine_tiles.shape[-1]
    slots = rest[1].shape[0]
    tile_bytes = 2 * n_grp * slots * tile_size * tile_size * 2
    fits = tile_bytes + 4 * orbitals.size * 2 < VMEM_LIMIT
    even = orbital_count % (n_grp * ROW_TILE) == 0 and tile_size % 128 == 0
    paired = n_col % 2 == 0 and slots == n_col and slots <= 128
    if fits and even and paired and n_grp == 4 and n_col > 2:
        return exchange_plan(n_grp, n_col, orbitals, cosine_tiles, *rest)
    return gather_plan(orbitals, cosine_tiles, *rest)


def solution(mesh):
    in_specs = (
        P(None, "col", "grp"),
        P(("grp", "col"), None, None),
        P(("grp", "col"), None, None),
        P("grp"),
        P("grp"),
        P(),
    )
    out_specs = P(None, "col", "grp")
    return jax.shard_map(
        functools.partial(on_device, mesh.shape["grp"], mesh.shape["col"]),
        mesh=mesh,
        in_specs=in_specs,
        out_specs=out_specs,
        check_vma=False,
    )
```

```python
import functools

import jax
import jax.numpy as jnp
from jax import lax
from jax.experimental import pallas as pl
from jax.experimental.pallas import tpu as pltpu
from jax.sharding import PartitionSpec as P

STEPS = 2
ROW_TILE = 16
CHUNKS = 3
MESH = pl.DeviceIdType.MESH
VMEM_LIMIT = 48 * 2**20


def row_sums(product, rows_onehot):
    group_rows = rows_onehot.shape[1]
    totals = [
        jnp.sum(product * rows_onehot[:, row_number][None, :, None], axis=1)
        for row_number in range(group_rows)
    ]
    return jnp.stack(totals, axis=1)


def tile_product(panels, tiles, rows_onehot, source):
    chosen = jnp.take(panels, source, axis=1)
    product = jnp.einsum("osj,sij->osi", chosen, tiles, preferred_element_type=jnp.float32)
    return row_sums(product, rows_onehot)


def find_source(tile_col, row_place):
    blocks = jnp.arange(row_place.shape[0], dtype=jnp.int32)
    return jnp.sum(jnp.where(tile_col[:, None] == blocks[None, :], row_place[None, :], 0), axis=1)


def gather_plan(orbitals, cosine_tiles, sine_tiles, tile_row, tile_col, row_place):
    halves, orbital_count, rows_dev = orbitals.shape
    tile_size = cosine_tiles.shape[-1]
    group_rows = rows_dev // tile_size
    slab_blocks = row_place.shape[0]
    columns = halves * orbital_count
    source = find_source(tile_col, row_place)
    rows_onehot = (tile_row[:, None] == jnp.arange(group_rows, dtype=jnp.int32)[None, :]).astype(
        jnp.float32
    )
    current = orbitals
    cosine_all = lax.all_gather(cosine_tiles, "col", axis=0, tiled=True)
    sine_all = lax.all_gather(sine_tiles, "col", axis=0, tiled=True)
    for _ in range(STEPS):
        panels = lax.all_gather(current, "grp", axis=2, tiled=True).reshape(
            columns, slab_blocks, tile_size
        )
        direct = tile_product(panels, cosine_all, rows_onehot, source)
        spread = direct.astype(jnp.bfloat16).reshape(halves, orbital_count, rows_dev)
        spread_all = lax.all_gather(spread, "grp", axis=2, tiled=True).reshape(
            columns, slab_blocks, tile_size
        )
        cosine_part = tile_product(spread_all, cosine_all, rows_onehot, source)
        sine_part = tile_product(spread_all, sine_all, rows_onehot, source)
        previous = current.astype(jnp.float32).reshape(columns, group_rows, tile_size)
        real_new = (
            2.0 * (cosine_part[:orbital_count] + sine_part[orbital_count:])
            - previous[:orbital_count]
        )
        imag_new = (
            2.0 * (cosine_part[orbital_count:] - sine_part[:orbital_count])
            - previous[orbital_count:]
        )
        current = (
            jnp.concatenate([real_new, imag_new], axis=0)
            .astype(jnp.bfloat16)
            .reshape(halves, orbital_count, rows_dev)
        )
    return current


def slot_lists(tile_row, tile_col, row_place, group_rows):
    slots = tile_row.shape[0]
    number = jnp.arange(slots, dtype=jnp.int32)
    row = jnp.where(tile_row < 0, group_rows, tile_row)
    key = row * slots + number
    rank = jnp.sum((key[None, :] < key[:, None]).astype(jnp.int32), axis=1)
    place = (rank[None, :] == number[:, None]).astype(jnp.int32)
    source = find_source(tile_col, row_place)
    order = jnp.sum(place * number[None, :], axis=1)
    sorted_source = jnp.sum(place * source[None, :], axis=1)
    sorted_row = jnp.sum(place * row[None, :], axis=1)
    before = jnp.concatenate([jnp.full((1,), -1, jnp.int32), sorted_row[:-1]])
    keep = (sorted_row == before).astype(jnp.int32)
    rows = jnp.arange(group_rows, dtype=jnp.int32)
    last = jnp.maximum(jnp.sum((row[None, :] <= rows[:, None]).astype(jnp.int32), axis=1) - 1, 0)
    used = jnp.max((row[None, :] == rows[:, None]).astype(jnp.int32), axis=1)
    table = [order, sorted_source, keep, last, used]
    table = [jnp.pad(line, (0, 128 - line.shape[0])) for line in table]
    return jnp.pad(jnp.stack(table), ((0, 8 - len(table)), (0, 0)))


def dot(panel, tile):
    return jnp.dot(panel, tile, preferred_element_type=jnp.float32)


def stages(current, spread, sums, tiles, table, group_rows, slots):
    halves, length, tile_size = current.shape[1:]
    height = halves * length

    def slot_values(g, k):
        return table[g, 0, k], table[g, 1, k], table[g, 2, k].astype(jnp.float32)

    def spread_group(g, carry):
        total = None
        for k in range(slots):
            slot, source, keep = slot_values(g, k)
            panel = current[source].reshape(height, tile_size)
            product = dot(panel, tiles[g, slot, :tile_size])
            total = product if k == 0 else product + total * keep
            sums[k, :height] = total
        for r in range(group_rows):
            used = table[g, 4, r].astype(jnp.float32)
            rows = (sums[table[g, 3, r], :height] * used).astype(spread.dtype)
            block = g * group_rows + r
            spread[block, :height, :tile_size] = rows
            spread[block, :length, tile_size:] = rows[length:]
            spread[block, length:height, tile_size:] = -rows[:length]
        return carry

    def double_group(g, carry):
        total = None
        for k in range(slots):
            slot, source, keep = slot_values(g, k)
            product = dot(spread[source, :height], tiles[g, slot])
            total = product if k == 0 else product + total * keep
            sums[k, :height] = total
        for r in range(group_rows):
            used = table[g, 4, r].astype(jnp.float32)
            block = g * group_rows + r
            previous = current[block].reshape(height, tile_size).astype(jnp.float32)
            new = 2.0 * (sums[table[g, 3, r], :height] * used) - previous
            current[block] = new.astype(current.dtype).reshape(halves, length, tile_size)
        return carry

    return spread_group, double_group


def kernel(n_grp, n_z, cuts, group_rows, orb, cos_in, sin_in, lists, out, *scratch):
    currents = scratch[: len(cuts)]
    (
        spread,
        sums,
        tiles,
        table_v,
        table,
        list_send,
        list_recv,
        table_sem,
        lane_send,
        lane_recv,
        pair_send,
        pair_recv,
        own_sem,
        in_send,
        in_recv,
        in_local,
        out_send,
        out_recv,
        out_local,
    ) = scratch[len(cuts) :]
    tile_size = tiles.shape[-1]
    slots = tiles.shape[1]
    share = orb.shape[1] // n_grp
    grp, col = lax.axis_index("grp"), lax.axis_index("col")
    z, core = col // 2, col % 2

    def grp_at(diff):
        return lax.rem(grp // 2 + diff // 2, 2) * 2 + lax.rem(grp + diff, 2)

    def z_at(shift):
        return lax.rem(z + shift + n_z, n_z)

    def device(dg, dz):
        return (grp_at(dg), z_at(dz) * 2 + core)

    pair = (grp, z * 2 + 1 - core)
    sent = []

    def remote(src, dst, send_sem, recv_sem, to):
        return pltpu.make_async_remote_copy(
            src_ref=src,
            dst_ref=dst,
            send_sem=send_sem,
            recv_sem=recv_sem,
            device_id=to,
            device_id_type=MESH,
        )

    def start(copy):
        copy.start()
        sent.append(copy)

    barrier = pltpu.get_barrier_semaphore()
    partners = [device(s, 0) for s in range(1, n_grp)]
    partners += [device(0, s) for s in range(1, n_z)] + [pair]
    for partner in partners:
        pl.semaphore_signal(barrier, inc=1, device_id=partner, device_id_type=MESH)
    tiles[grp, col, :tile_size] = cos_in[0].T
    tiles[grp, col, tile_size:] = sin_in[0].T
    pl.semaphore_wait(barrier, len(partners))

    def tile_ref(k, tg, tz, lane):
        place = grp_at(tg), z_at(-tz) * 2 + lane
        return tiles.at[place[0], place[1], pl.ds(k * tile_size, tile_size)]

    def lane_copy(k, tg, tz, dg, dz):
        dst = tile_ref(k, tg, tz, core)
        at = (k, tg ^ dg, (tz + dz) % n_z)
        return remote(dst, dst, lane_send.at[at], lane_recv.at[at], device(dg, dz))

    def lane_wait(k, sg, sz):
        ref = tile_ref(k, sg, sz, core)
        at = (k, sg, sz)
        remote(ref, ref, lane_send.at[at], lane_recv.at[at], pair).wait_recv()

    def pair_copy(k, sg, sz):
        dst = tile_ref(k, sg, sz, core)
        at = (k, sg, sz)
        start(remote(dst, dst, pair_send.at[at], pair_recv.at[at], pair))

    def pair_wait(k, sg, sz):
        ref = tile_ref(k, sg, sz, 1 - core)
        at = (k, sg, sz)
        remote(ref, ref, pair_send.at[at], pair_recv.at[at], pair).wait_recv()

    guarded = []

    def start_if(condition, copy):
        guarded.append((condition, copy))
        pl.when(condition)(copy.start)

    def pass_on(sg, sz):
        below = z >= sz
        up, down = z < n_z - 1, z > 0
        if sz:
            up, down = jnp.logical_and(up, below), jnp.logical_and(down, jnp.logical_not(below))
        start_if(up, lane_copy(1, sg, sz, 0, 1))
        start_if(down, lane_copy(1, sg, sz, 0, -1))

    others = range(1, n_grp)
    for s in others:
        start(remote(lists, table_v.at[grp], list_send.at[s], list_recv.at[s], device(s, 0)))
    for s in others:
        start(lane_copy(1, 0, 0, s, 0))
    for s in range(1, n_z):
        start(lane_copy(0, 0, 0, 0, s))
    pass_on(0, 0)
    own_lists = pltpu.make_async_copy(lists, table_v.at[grp], own_sem.at[0])
    own_lists.start()
    for k in range(2):
        pair_copy(k, 0, 0)
    for s in (1, 2):
        start(lane_copy(0, 0, 0, s, 0))

    def in_piece(c, s, r):
        begin, length = cuts[c]
        rows = pl.ds(pl.multiple_of(grp_at(s) * share + begin, ROW_TILE), length)
        src = orb.at[:, rows, pl.ds(r * tile_size, tile_size)]
        return src, currents[c].at[grp * group_rows + r]

    def send_orbitals(c):
        for r in range(group_rows):
            src, dst = in_piece(c, 0, r)
            pltpu.make_async_copy(src, dst, in_local.at[c, r]).start()
            for s in (3, 1, 2):
                src, dst = in_piece(c, s, r)
                at = (c, s, r)
                start(remote(src, dst, in_send.at[at], in_recv.at[at], device(s, 0)))

    send_orbitals(0)

    near = sorted(range(1, n_z), key=lambda s: (min(s, n_z - s), s))
    for i in range(max(n_grp, n_z) - 1):
        if i < n_z - 1:
            lane_wait(0, 0, near[i])
            for d in (1, 2):
                start(lane_copy(0, 0, near[i], d, 0))
            pair_copy(0, 0, near[i])
        if i < n_grp - 1:
            lane_wait(1, i + 1, 0)
            pass_on(i + 1, 0)
            pair_copy(1, i + 1, 0)
    def cosine_across(sz):
        for d in (1, 2):
            lane_wait(0, d, sz)
            if d == 1 + sz % 2:
                start(lane_copy(0, d, sz, 3 - d, 0))
            pair_copy(0, d, sz)

    def sine_along(sz):
        for sg in range(n_grp):
            lane_wait(1, sg, sz)
            pass_on(sg, sz)
            pair_copy(1, sg, sz)

    cosine_across(0)
    for sz in near[:2]:
        sine_along(sz)
    for sz in near:
        cosine_across(sz)
    for c in range(1, len(cuts)):
        send_orbitals(c)
    for sz in near[2:]:
        sine_along(sz)
    for sz in [0] + near:
        lane_wait(0, 3, sz)
        pair_copy(0, 3, sz)
    own_lists.wait()
    for s in others:
        ref = table_v.at[grp_at(s)]
        remote(ref, ref, list_send.at[s], list_recv.at[s], pair).wait_recv()
    to_scalar = pltpu.make_async_copy(table_v, table, table_sem.at[0])
    to_scalar.start()
    to_scalar.wait()

    def pair_waits(k):
        for sg in range(n_grp):
            for sz in range(n_z):
                pair_wait(k, sg, sz)

    def out_piece(c, s, r):
        begin, length = cuts[c]
        rows = pl.ds(pl.multiple_of(grp * share + begin, ROW_TILE), length)
        dst = out.at[:, rows, pl.ds(r * tile_size, tile_size)]
        return currents[c].at[grp_at(s) * group_rows + r], dst

    def landing(c, s, r):
        begin, length = cuts[c]
        rows = pl.ds(pl.multiple_of(grp_at(s) * share + begin, ROW_TILE), length)
        return out.at[:, rows, pl.ds(r * tile_size, tile_size)]

    for c in range(len(cuts)):
        for r in range(group_rows):
            src, dst = in_piece(c, 0, r)
            pltpu.make_async_copy(src, dst, in_local.at[c, r]).wait()
            for s in range(1, n_grp):
                ref = currents[c].at[grp_at(s) * group_rows + r]
                at = (c, s, r)
                remote(ref, ref, in_send.at[at], in_recv.at[at], pair).wait_recv()
        spread_group, double_group = stages(
            currents[c], spread, sums, tiles, table, group_rows, slots
        )
        if c == 0:
            pair_waits(0)
            pair_waits(1)
        lax.fori_loop(0, n_grp, spread_group, 0)
        def step(_, carry):
            lax.fori_loop(0, n_grp, double_group, 0)
            lax.fori_loop(0, n_grp, spread_group, 0)
            return carry

        lax.fori_loop(0, STEPS - 1, step, 0)
        for s in (3, 1, 2, 0):
            double_group(grp_at(s), 0)
            for r in range(group_rows):
                src, dst = out_piece(c, s, r)
                if s == 0:
                    pltpu.make_async_copy(src, dst, out_local.at[c, r]).start()
                else:
                    at = (c, s, r)
                    start(remote(src, dst, out_send.at[at], out_recv.at[at], device(s, 0)))
    for c in range(len(cuts)):
        for r in range(group_rows):
            src, dst = out_piece(c, 0, r)
            pltpu.make_async_copy(src, dst, out_local.at[c, r]).wait()
            for s in range(1, n_grp):
                ref = landing(c, s, r)
                at = (c, s, r)
                remote(ref, ref, out_send.at[at], out_recv.at[at], pair).wait_recv()
    for copy in sent:
        copy.wait_send()
    for condition, copy in guarded:
        pl.when(condition)(copy.wait_send)


def chunk_cuts(share):
    pieces = share // ROW_TILE
    count = min(CHUNKS, pieces)
    sizes = [(pieces // count + (c < pieces % count)) * ROW_TILE for c in range(count)]
    return [(sum(sizes[:c]), sizes[c]) for c in range(count)]


def exchange_plan(n_grp, n_col, orbitals, cosine_tiles, sine_tiles, tile_row, tile_col, row_place):
    halves, orbital_count, rows_dev = orbitals.shape
    tile_size = cosine_tiles.shape[-1]
    group_rows = rows_dev // tile_size
    slots = tile_row.shape[0]
    blocks = row_place.shape[0]
    n_z = n_col // 2
    cuts = chunk_cuts(orbital_count // n_grp)
    tallest = halves * max(length for _, length in cuts)
    lists = slot_lists(tile_row, tile_col, row_place, group_rows)
    dma = pltpu.SemaphoreType.DMA
    grid = (len(cuts), n_grp, group_rows)
    scratch = [
        pltpu.VMEM((blocks, halves, length, tile_size), orbitals.dtype) for _, length in cuts
    ]
    scratch += [
        pltpu.VMEM((blocks, tallest, 2 * tile_size), jnp.bfloat16),
        pltpu.VMEM((slots, tallest, tile_size), jnp.float32),
        pltpu.VMEM((n_grp, slots, 2 * tile_size, tile_size), cosine_tiles.dtype),
        pltpu.VMEM((n_grp,) + lists.shape, jnp.int32),
        pltpu.SMEM((n_grp,) + lists.shape, jnp.int32),
        dma((n_grp,)),
        dma((n_grp,)),
        dma((1,)),
        dma((2, n_grp, n_z)),
        dma((2, n_grp, n_z)),
        dma((2, n_grp, n_z)),
        dma((2, n_grp, n_z)),
        dma((1,)),
        dma(grid),
        dma(grid),
        dma((len(cuts), group_rows)),
        dma(grid),
        dma(grid),
        dma((len(cuts), group_rows)),
    ]
    return pl.pallas_call(
        functools.partial(kernel, n_grp, n_z, cuts, group_rows),
        out_shape=jax.ShapeDtypeStruct(orbitals.shape, orbitals.dtype),
        in_specs=[pl.BlockSpec(memory_space=space) for space in (pltpu.HBM, pltpu.VMEM, pltpu.VMEM, pltpu.HBM)],
        out_specs=pl.BlockSpec(memory_space=pl.ANY),
        scratch_shapes=scratch,
        compiler_params=pltpu.CompilerParams(
            collective_id=0, has_side_effects=True, vmem_limit_bytes=VMEM_LIMIT
        ),
    )(orbitals, cosine_tiles, sine_tiles, lists)


def on_device(n_grp, n_col, orbitals, cosine_tiles, *rest):
    halves, orbital_count, rows_dev = orbitals.shape
    tile_size = cosine_tiles.shape[-1]
    slots = rest[1].shape[0]
    tile_bytes = 2 * n_grp * slots * tile_size * tile_size * 2
    fits = tile_bytes + 4 * orbitals.size * 2 < VMEM_LIMIT
    even = orbital_count % (n_grp * ROW_TILE) == 0 and tile_size % 128 == 0
    paired = n_col % 2 == 0 and slots == n_col and slots <= 128
    if fits and even and paired and n_grp == 4 and n_col > 2:
        return exchange_plan(n_grp, n_col, orbitals, cosine_tiles, *rest)
    return gather_plan(orbitals, cosine_tiles, *rest)


def solution(mesh):
    in_specs = (
        P(None, "col", "grp"),
        P(("grp", "col"), None, None),
        P(("grp", "col"), None, None),
        P("grp"),
        P("grp"),
        P(),
    )
    out_specs = P(None, "col", "grp")
    return jax.shard_map(
        functools.partial(on_device, mesh.shape["grp"], mesh.shape["col"]),
        mesh=mesh,
        in_specs=in_specs,
        out_specs=out_specs,
        check_vma=False,
    )
```

```python
import functools

import jax
import jax.numpy as jnp
from jax import lax
from jax.experimental import pallas as pl
from jax.experimental.pallas import tpu as pltpu
from jax.sharding import PartitionSpec as P

STEPS = 2
ROW_TILE = 16
CHUNKS = 3
MESH = pl.DeviceIdType.MESH
VMEM_LIMIT = 63 * 2**20


def row_sums(product, rows_onehot):
    group_rows = rows_onehot.shape[1]
    totals = [
        jnp.sum(product * rows_onehot[:, row_number][None, :, None], axis=1)
        for row_number in range(group_rows)
    ]
    return jnp.stack(totals, axis=1)


def tile_product(panels, tiles, rows_onehot, source):
    chosen = jnp.take(panels, source, axis=1)
    product = jnp.einsum("osj,sij->osi", chosen, tiles, preferred_element_type=jnp.float32)
    return row_sums(product, rows_onehot)


def find_source(tile_col, row_place):
    blocks = jnp.arange(row_place.shape[0], dtype=jnp.int32)
    return jnp.sum(jnp.where(tile_col[:, None] == blocks[None, :], row_place[None, :], 0), axis=1)


def gather_plan(orbitals, cosine_tiles, sine_tiles, tile_row, tile_col, row_place):
    halves, orbital_count, rows_dev = orbitals.shape
    tile_size = cosine_tiles.shape[-1]
    group_rows = rows_dev // tile_size
    slab_blocks = row_place.shape[0]
    columns = halves * orbital_count
    source = find_source(tile_col, row_place)
    rows_onehot = (tile_row[:, None] == jnp.arange(group_rows, dtype=jnp.int32)[None, :]).astype(
        jnp.float32
    )
    current = orbitals
    cosine_all = lax.all_gather(cosine_tiles, "col", axis=0, tiled=True)
    sine_all = lax.all_gather(sine_tiles, "col", axis=0, tiled=True)
    for _ in range(STEPS):
        panels = lax.all_gather(current, "grp", axis=2, tiled=True).reshape(
            columns, slab_blocks, tile_size
        )
        direct = tile_product(panels, cosine_all, rows_onehot, source)
        spread = direct.astype(jnp.bfloat16).reshape(halves, orbital_count, rows_dev)
        spread_all = lax.all_gather(spread, "grp", axis=2, tiled=True).reshape(
            columns, slab_blocks, tile_size
        )
        cosine_part = tile_product(spread_all, cosine_all, rows_onehot, source)
        sine_part = tile_product(spread_all, sine_all, rows_onehot, source)
        previous = current.astype(jnp.float32).reshape(columns, group_rows, tile_size)
        real_new = (
            2.0 * (cosine_part[:orbital_count] + sine_part[orbital_count:])
            - previous[:orbital_count]
        )
        imag_new = (
            2.0 * (cosine_part[orbital_count:] - sine_part[:orbital_count])
            - previous[orbital_count:]
        )
        current = (
            jnp.concatenate([real_new, imag_new], axis=0)
            .astype(jnp.bfloat16)
            .reshape(halves, orbital_count, rows_dev)
        )
    return current


def slot_lists(tile_row, tile_col, row_place, group_rows):
    slots = tile_row.shape[0]
    number = jnp.arange(slots, dtype=jnp.int32)
    row = jnp.where(tile_row < 0, group_rows, tile_row)
    key = row * slots + number
    rank = jnp.sum((key[None, :] < key[:, None]).astype(jnp.int32), axis=1)
    place = (rank[None, :] == number[:, None]).astype(jnp.int32)
    source = find_source(tile_col, row_place)
    order = jnp.sum(place * number[None, :], axis=1)
    sorted_source = jnp.sum(place * source[None, :], axis=1)
    sorted_row = jnp.sum(place * row[None, :], axis=1)
    before = jnp.concatenate([jnp.full((1,), -1, jnp.int32), sorted_row[:-1]])
    keep = (sorted_row == before).astype(jnp.int32)
    rows = jnp.arange(group_rows, dtype=jnp.int32)
    last = jnp.maximum(jnp.sum((row[None, :] <= rows[:, None]).astype(jnp.int32), axis=1) - 1, 0)
    used = jnp.max((row[None, :] == rows[:, None]).astype(jnp.int32), axis=1)
    table = [order, sorted_source, keep, last, used]
    table = [jnp.pad(line, (0, 128 - line.shape[0])) for line in table]
    return jnp.pad(jnp.stack(table), ((0, 8 - len(table)), (0, 0)))


def dot(panel, tile):
    return jnp.dot(panel, tile, preferred_element_type=jnp.float32)


def stages(current, spread, sums, tiles, table, group_rows, slots):
    halves, length, tile_size = current.shape[1:]
    height = halves * length

    def slot_values(g, k):
        return table[g, 0, k], table[g, 1, k], table[g, 2, k].astype(jnp.float32)

    def spread_group(g, carry):
        total = None
        for k in range(slots):
            slot, source, keep = slot_values(g, k)
            panel = current[source].reshape(height, tile_size)
            product = dot(panel, tiles[g, slot, :tile_size])
            total = product if k == 0 else product + total * keep
            sums[k, :height] = total
        for r in range(group_rows):
            used = table[g, 4, r].astype(jnp.float32)
            rows = (sums[table[g, 3, r], :height] * used).astype(spread.dtype)
            block = g * group_rows + r
            spread[block, :height, :tile_size] = rows
            spread[block, :length, tile_size:] = rows[length:]
            spread[block, length:height, tile_size:] = -rows[:length]
        return carry

    def double_group(g, carry):
        total = None
        for k in range(slots):
            slot, source, keep = slot_values(g, k)
            product = dot(spread[source, :height], tiles[g, slot])
            total = product if k == 0 else product + total * keep
            sums[k, :height] = total
        for r in range(group_rows):
            used = table[g, 4, r].astype(jnp.float32)
            block = g * group_rows + r
            previous = current[block].reshape(height, tile_size).astype(jnp.float32)
            new = 2.0 * (sums[table[g, 3, r], :height] * used) - previous
            current[block] = new.astype(current.dtype).reshape(halves, length, tile_size)
        return carry

    return spread_group, double_group


def kernel(n_grp, n_z, cuts, group_rows, orb, cos_in, sin_in, lists, out, *scratch):
    currents = scratch[: len(cuts)]
    (
        spread,
        sums,
        tiles,
        table_v,
        table,
        list_send,
        list_recv,
        table_sem,
        lane_send,
        lane_recv,
        pair_send,
        pair_recv,
        own_sem,
        in_send,
        in_recv,
        in_local,
        out_send,
        out_recv,
        out_local,
    ) = scratch[len(cuts) :]
    tile_size = tiles.shape[-1]
    slots = tiles.shape[1]
    share = orb.shape[1] // n_grp
    grp, col = lax.axis_index("grp"), lax.axis_index("col")
    z, core = col // 2, col % 2

    def grp_at(diff):
        return lax.rem(grp // 2 + diff // 2, 2) * 2 + lax.rem(grp + diff, 2)

    def z_at(shift):
        return lax.rem(z + shift + n_z, n_z)

    def device(dg, dz):
        return (grp_at(dg), z_at(dz) * 2 + core)

    pair = (grp, z * 2 + 1 - core)
    sent = []

    def remote(src, dst, send_sem, recv_sem, to):
        return pltpu.make_async_remote_copy(
            src_ref=src,
            dst_ref=dst,
            send_sem=send_sem,
            recv_sem=recv_sem,
            device_id=to,
            device_id_type=MESH,
        )

    def start(copy):
        copy.start()
        sent.append(copy)

    barrier = pltpu.get_barrier_semaphore()
    partners = [device(s, 0) for s in range(1, n_grp)]
    partners += [device(0, s) for s in range(1, n_z)] + [pair]
    for partner in partners:
        pl.semaphore_signal(barrier, inc=1, device_id=partner, device_id_type=MESH)
    tiles[grp, col, :tile_size] = cos_in[0].T
    tiles[grp, col, tile_size:] = sin_in[0].T
    pl.semaphore_wait(barrier, len(partners))

    def tile_ref(k, tg, tz, lane):
        place = grp_at(tg), z_at(-tz) * 2 + lane
        return tiles.at[place[0], place[1], pl.ds(k * tile_size, tile_size)]

    def lane_copy(k, tg, tz, dg, dz):
        dst = tile_ref(k, tg, tz, core)
        at = (k, tg ^ dg, (tz + dz) % n_z)
        return remote(dst, dst, lane_send.at[at], lane_recv.at[at], device(dg, dz))

    def lane_wait(k, sg, sz):
        ref = tile_ref(k, sg, sz, core)
        at = (k, sg, sz)
        remote(ref, ref, lane_send.at[at], lane_recv.at[at], pair).wait_recv()

    def pair_copy(k, sg, sz):
        dst = tile_ref(k, sg, sz, core)
        at = (k, sg, sz)
        start(remote(dst, dst, pair_send.at[at], pair_recv.at[at], pair))

    def pair_wait(k, sg, sz):
        ref = tile_ref(k, sg, sz, 1 - core)
        at = (k, sg, sz)
        remote(ref, ref, pair_send.at[at], pair_recv.at[at], pair).wait_recv()

    guarded = []

    def start_if(condition, copy):
        guarded.append((condition, copy))
        pl.when(condition)(copy.start)

    def pass_on(sg, sz):
        below = z >= sz
        up, down = z < n_z - 1, z > 0
        if sz:
            up, down = jnp.logical_and(up, below), jnp.logical_and(down, jnp.logical_not(below))
        start_if(up, lane_copy(1, sg, sz, 0, 1))
        start_if(down, lane_copy(1, sg, sz, 0, -1))

    others = range(1, n_grp)
    for s in others:
        start(remote(lists, table_v.at[grp], list_send.at[s], list_recv.at[s], device(s, 0)))
    for s in others:
        start(lane_copy(1, 0, 0, s, 0))
    for s in range(1, n_z):
        start(lane_copy(0, 0, 0, 0, s))
    pass_on(0, 0)
    own_lists = pltpu.make_async_copy(lists, table_v.at[grp], own_sem.at[0])
    own_lists.start()
    for k in range(2):
        pair_copy(k, 0, 0)
    for s in (1, 2):
        start(lane_copy(0, 0, 0, s, 0))

    def in_piece(c, s, r):
        begin, length = cuts[c]
        rows = pl.ds(pl.multiple_of(grp_at(s) * share + begin, ROW_TILE), length)
        src = orb.at[:, rows, pl.ds(r * tile_size, tile_size)]
        return src, currents[c].at[grp * group_rows + r]

    def send_orbitals(c):
        for r in range(group_rows):
            src, dst = in_piece(c, 0, r)
            pltpu.make_async_copy(src, dst, in_local.at[c, r]).start()
            for s in (3, 1, 2):
                src, dst = in_piece(c, s, r)
                at = (c, s, r)
                start(remote(src, dst, in_send.at[at], in_recv.at[at], device(s, 0)))

    send_orbitals(0)

    near = sorted(range(1, n_z), key=lambda s: (min(s, n_z - s), s))
    for i in range(max(n_grp, n_z) - 1):
        if i < n_z - 1:
            lane_wait(0, 0, near[i])
            for d in (1, 2):
                start(lane_copy(0, 0, near[i], d, 0))
            pair_copy(0, 0, near[i])
        if i < n_grp - 1:
            lane_wait(1, i + 1, 0)
            pass_on(i + 1, 0)
            pair_copy(1, i + 1, 0)
    for c in range(1, len(cuts)):
        send_orbitals(c)

    def cosine_across(sz):
        for d in (1, 2):
            lane_wait(0, d, sz)
            if d == 1 + sz % 2:
                start(lane_copy(0, d, sz, 3 - d, 0))
            pair_copy(0, d, sz)

    def sine_along(sz):
        for sg in range(n_grp):
            lane_wait(1, sg, sz)
            pass_on(sg, sz)
            pair_copy(1, sg, sz)

    cosine_across(0)
    for sz in near[:2]:
        sine_along(sz)
    for sz in near:
        cosine_across(sz)
    for sz in near[2:]:
        sine_along(sz)
    for sz in [0] + near:
        lane_wait(0, 3, sz)
        pair_copy(0, 3, sz)
    own_lists.wait()
    for s in others:
        ref = table_v.at[grp_at(s)]
        remote(ref, ref, list_send.at[s], list_recv.at[s], pair).wait_recv()
    to_scalar = pltpu.make_async_copy(table_v, table, table_sem.at[0])
    to_scalar.start()
    to_scalar.wait()

    def pair_waits(k):
        for sg in range(n_grp):
            for sz in range(n_z):
                pair_wait(k, sg, sz)

    def out_piece(c, s, r):
        begin, length = cuts[c]
        rows = pl.ds(pl.multiple_of(grp * share + begin, ROW_TILE), length)
        dst = out.at[:, rows, pl.ds(r * tile_size, tile_size)]
        return currents[c].at[grp_at(s) * group_rows + r], dst

    def landing(c, s, r):
        begin, length = cuts[c]
        rows = pl.ds(pl.multiple_of(grp_at(s) * share + begin, ROW_TILE), length)
        return out.at[:, rows, pl.ds(r * tile_size, tile_size)]

    for c in range(len(cuts)):
        for r in range(group_rows):
            src, dst = in_piece(c, 0, r)
            pltpu.make_async_copy(src, dst, in_local.at[c, r]).wait()
            for s in range(1, n_grp):
                ref = currents[c].at[grp_at(s) * group_rows + r]
                at = (c, s, r)
                remote(ref, ref, in_send.at[at], in_recv.at[at], pair).wait_recv()
        spread_group, double_group = stages(
            currents[c], spread, sums, tiles, table, group_rows, slots
        )
        if c == 0:
            pair_waits(0)
            pair_waits(1)
        lax.fori_loop(0, n_grp, spread_group, 0)
        def step(_, carry):
            lax.fori_loop(0, n_grp, double_group, 0)
            lax.fori_loop(0, n_grp, spread_group, 0)
            return carry

        lax.fori_loop(0, STEPS - 1, step, 0)
        for s in (3, 1, 2, 0):
            double_group(grp_at(s), 0)
            for r in range(group_rows):
                src, dst = out_piece(c, s, r)
                if s == 0:
                    pltpu.make_async_copy(src, dst, out_local.at[c, r]).start()
                else:
                    at = (c, s, r)
                    start(remote(src, dst, out_send.at[at], out_recv.at[at], device(s, 0)))
    for c in range(len(cuts)):
        for r in range(group_rows):
            src, dst = out_piece(c, 0, r)
            pltpu.make_async_copy(src, dst, out_local.at[c, r]).wait()
            for s in range(1, n_grp):
                ref = landing(c, s, r)
                at = (c, s, r)
                remote(ref, ref, out_send.at[at], out_recv.at[at], pair).wait_recv()
    for copy in sent:
        copy.wait_send()
    for condition, copy in guarded:
        pl.when(condition)(copy.wait_send)


def chunk_cuts(share):
    pieces = share // ROW_TILE
    count = min(CHUNKS, pieces)
    sizes = [(pieces // count + (c < pieces % count)) * ROW_TILE for c in range(count)]
    return [(sum(sizes[:c]), sizes[c]) for c in range(count)]


def exchange_plan(n_grp, n_col, orbitals, cosine_tiles, sine_tiles, tile_row, tile_col, row_place):
    halves, orbital_count, rows_dev = orbitals.shape
    tile_size = cosine_tiles.shape[-1]
    group_rows = rows_dev // tile_size
    slots = tile_row.shape[0]
    blocks = row_place.shape[0]
    n_z = n_col // 2
    cuts = chunk_cuts(orbital_count // n_grp)
    tallest = halves * max(length for _, length in cuts)
    lists = slot_lists(tile_row, tile_col, row_place, group_rows)
    dma = pltpu.SemaphoreType.DMA
    grid = (len(cuts), n_grp, group_rows)
    scratch = [
        pltpu.VMEM((blocks, halves, length, tile_size), orbitals.dtype) for _, length in cuts
    ]
    scratch += [
        pltpu.VMEM((blocks, tallest, 2 * tile_size), jnp.bfloat16),
        pltpu.VMEM((slots, tallest, tile_size), jnp.float32),
        pltpu.VMEM((n_grp, slots, 2 * tile_size, tile_size), cosine_tiles.dtype),
        pltpu.VMEM((n_grp,) + lists.shape, jnp.int32),
        pltpu.SMEM((n_grp,) + lists.shape, jnp.int32),
        dma((n_grp,)),
        dma((n_grp,)),
        dma((1,)),
        dma((2, n_grp, n_z)),
        dma((2, n_grp, n_z)),
        dma((2, n_grp, n_z)),
        dma((2, n_grp, n_z)),
        dma((1,)),
        dma(grid),
        dma(grid),
        dma((len(cuts), group_rows)),
        dma(grid),
        dma(grid),
        dma((len(cuts), group_rows)),
    ]
    return pl.pallas_call(
        functools.partial(kernel, n_grp, n_z, cuts, group_rows),
        out_shape=jax.ShapeDtypeStruct(orbitals.shape, orbitals.dtype),
        in_specs=[pl.BlockSpec(memory_space=space) for space in (pltpu.HBM, pltpu.VMEM, pltpu.VMEM, pltpu.HBM)],
        out_specs=pl.BlockSpec(memory_space=pl.ANY),
        scratch_shapes=scratch,
        compiler_params=pltpu.CompilerParams(
            collective_id=0, has_side_effects=True, vmem_limit_bytes=VMEM_LIMIT
        ),
    )(orbitals, cosine_tiles, sine_tiles, lists)


def on_device(n_grp, n_col, orbitals, cosine_tiles, *rest):
    halves, orbital_count, rows_dev = orbitals.shape
    tile_size = cosine_tiles.shape[-1]
    slots = rest[1].shape[0]
    tile_bytes = 2 * n_grp * slots * tile_size * tile_size * 2
    fits = tile_bytes + 4 * orbitals.size * 2 < VMEM_LIMIT
    even = orbital_count % (n_grp * ROW_TILE) == 0 and tile_size % 128 == 0
    paired = n_col % 2 == 0 and slots == n_col and slots <= 128
    if fits and even and paired and n_grp == 4 and n_col > 2:
        return exchange_plan(n_grp, n_col, orbitals, cosine_tiles, *rest)
    return gather_plan(orbitals, cosine_tiles, *rest)


def solution(mesh):
    in_specs = (
        P(None, "col", "grp"),
        P(("grp", "col"), None, None),
        P(("grp", "col"), None, None),
        P("grp"),
        P("grp"),
        P(),
    )
    out_specs = P(None, "col", "grp")
    return jax.shard_map(
        functools.partial(on_device, mesh.shape["grp"], mesh.shape["col"]),
        mesh=mesh,
        in_specs=in_specs,
        out_specs=out_specs,
        check_vma=False,
    )
```
